32 devices in a mesh: tenant: 2 (over x), row: 2 (over core), col: 8 (over z, y).
Axes of the slice: x: 2, y: 2, z: 4, core: 2. Of those that a mesh axis runs over, the one named last changes fastest.
Arguments:
- tokens: bfloat16 [2048, 8192], P(('tenant', 'row'), 'col'), parts along dimension 0, may hold values from -6 to 6
- base_weight: bfloat16 [8192, 28672], P('row', 'col'), may hold values from -0.0625 to 0.0625
- delta_values: bfloat16 [24576, 1024], P(('tenant', 'row'), 'col'), parts along dimension 0, may hold values from -0.29882812 to 0.29882812
- delta_index: int32 [192, 8], P(('tenant', 'row'), 'col'), parts along dimension 0, may hold values from 0 to 895, as said below
- delta_count: int32 [4, 8], P(('tenant', 'row'), 'col'), parts along dimension 0, may hold values from 12 to 48, as said below
Outputs:
- hidden: bfloat16 [2048, 28672], P(('tenant', 'row'), 'col'), parts along dimension 0
The draws below stay inside these ranges and needn't reach their ends.
There are 2 independent parts, one for each index of `tenant`. The reference program is written for one: setup_inputs(seed, part) draws one part's arguments, and reference() takes and returns one part's arrays. A program takes and returns all parts, laid end to end along the dimension named above; an argument that names none is the same for every part. Nothing has to cross between parts.
Inputs may be any that keep to these rules, and one draw needn't show every extreme that they name: `delta_index`: within one device's 48 slots the values are distinct. `delta_count`: some device uses all 48 slots in every draw.
All inputs are finite; a program needn't handle non-finite values.
Results may differ from the reference program's by a relative error of at most 0.0041.
Values may be sent and summed in bfloat16 or wider, within the bound.
No kernel may reach another device: no remote copies, remote signals or barrier semaphores. Data moves between devices by JAX's collectives and lax.ppermute only.
A program may use at most 320 MiB of HBM per device.

```python
import jax
import jax.numpy as jnp
from jax import lax

D = 8192
FF = 28672
BLOCK = 128
SLOTS = 48
TOKENS = 1024
RBH = 32
CBL = 28
N_ROW = 2
N_COL = 8


def swap_values(order, first, second):
    return jnp.where(order == first, second, jnp.where(order == second, first, order))


def draw_delta_index(key, part):
    key = jax.random.fold_in(key, 11)
    pick_key, perm_key = jax.random.split(key)
    subkeys = jax.random.split(perm_key, N_ROW * N_COL)
    orders = jax.vmap(lambda one: jax.random.permutation(one, RBH * CBL))(subkeys)
    target = jax.random.randint(pick_key, (), 0, N_ROW * N_COL)
    top_value = RBH * CBL - 1
    fixed = swap_values(orders, orders[:, 0:1], top_value)
    fixed = swap_values(fixed, fixed[:, 1:2], 0)
    pick = (jnp.arange(N_ROW * N_COL) == target)[:, None]
    orders = jnp.where(pick, fixed, orders)
    chosen = orders[:, :SLOTS]
    chosen = chosen.reshape(N_ROW, N_COL, SLOTS).transpose(0, 2, 1)
    return chosen.reshape(N_ROW * SLOTS, N_COL).astype(jnp.int32)


def draw_delta_count(key, part):
    key = jax.random.fold_in(key, 23)
    first, second, third = jax.random.split(key, 3)
    total = N_ROW * N_COL
    counts = jax.random.randint(first, (total,), SLOTS // 4, SLOTS + 1)
    busiest = jax.random.randint(second, (), 0, total)
    lightest = (busiest + 1 + jax.random.randint(third, (), 0, total - 1)) % total
    place = jnp.arange(total)
    counts = jnp.where(place == busiest, SLOTS, counts)
    counts = jnp.where(place == lightest, SLOTS // 4, counts)
    return counts.reshape(N_ROW, N_COL).astype(jnp.int32)


def levels(key, shape, pieces, smallest, high):
    def one(dim, blocks):
        draws = jax.random.uniform(jax.random.fold_in(jax.random.fold_in(key, 6), dim), (blocks,), jnp.float32, smallest / len(pieces), high / len(pieces))
        return jnp.repeat(jnp.exp(draws), shape[dim] // blocks).reshape((-1,) + (1,) * (len(shape) - dim - 1))

    loudness = one(*pieces[0])
    for cut in pieces[1:]:
        loudness = loudness * one(*cut)
    return loudness


def centred(key, shape, spread, most, cuts=(), held_as=jnp.bfloat16):
    array = spread * jax.random.normal(key, shape, jnp.float32)
    if cuts:
        array = array * levels(key, shape, cuts, -0.22, 0.18)
    return jnp.clip(array, -most, most).astype(held_as)


def setup_inputs(seed: int = 0, part: int = 0) -> dict:
    key_of = jax.random.split(jax.random.key(seed), 6)
    own_keys = jax.random.split(jax.random.fold_in(key_of[5], part), 6)
    return {
        "tokens": centred(own_keys[0], (TOKENS, D), 1.0, 6.0, ((0, 2), (1, 8))),
        "base_weight": centred(key_of[1], (D, FF), D ** -0.5, 0.0625, ((0, 2), (1, 8))),
        "delta_values": centred(own_keys[2], (N_ROW * SLOTS * BLOCK, N_COL * BLOCK), 0.05, 0.29882812, ((0, 2), (1, 8))),
        "delta_index": draw_delta_index(jax.random.fold_in(jax.random.fold_in(key_of[5], part), 71), part),
        "delta_count": draw_delta_count(jax.random.fold_in(jax.random.fold_in(key_of[5], part), 71), part),
    }


def reference(tokens, base_weight, delta_values, delta_index, delta_count):
    panel_width = FF // N_COL
    values = delta_values.reshape(N_ROW, SLOTS, BLOCK, N_COL, BLOCK).transpose(3, 0, 1, 2, 4)
    block_ids = delta_index.reshape(N_ROW, SLOTS, N_COL).transpose(2, 0, 1)
    used = delta_count.T

    def panel_fn(column):
        weights = lax.dynamic_slice_in_dim(base_weight, column * panel_width, panel_width, 1)
        slot_values = values[column]
        slot_ids = block_ids[column]
        slot_used = used[column]
        active = jnp.arange(SLOTS, dtype=jnp.int32)[None, :] < slot_used[:, None]
        row_block = jnp.arange(N_ROW, dtype=jnp.int32)[:, None] * RBH + slot_ids // CBL
        col_block = slot_ids % CBL
        scaled = slot_values.astype(jnp.float32) * active[:, :, None, None].astype(jnp.float32)
        block_grid = jnp.zeros((N_ROW * RBH, CBL, BLOCK, BLOCK), jnp.float32)
        block_grid = block_grid.at[row_block.reshape(-1), col_block.reshape(-1)].add(scaled.reshape(-1, BLOCK, BLOCK))
        delta_dense = block_grid.transpose(0, 2, 1, 3).reshape(D, panel_width)
        effective = (weights.astype(jnp.float32) + delta_dense).astype(jnp.bfloat16)
        return jnp.dot(tokens, effective, preferred_element_type=jnp.float32).astype(jnp.bfloat16)

    panels = lax.map(panel_fn, jnp.arange(N_COL, dtype=jnp.int32))
    return panels.transpose(1, 0, 2).reshape(TOKENS, FF)
```

```python
import functools

import jax
import jax.numpy as jnp
import numpy as np
from jax import lax
from jax.experimental import pallas as pl
from jax.experimental.pallas import tpu as pltpu
from jax.sharding import PartitionSpec as P

STREAMS = 2
W_SLOTS = 3


def ring_order(n):
    return list(range(0, n, 2)) + list(range(n - 1, 0, -2))


def plan(n):
    ring = ring_order(n)
    place = {c: k for k, c in enumerate(ring)}
    half = n // 2
    order = np.zeros((n, 2, half), np.int32)
    events = [(d, min(half, STREAMS * d)) for d in range(1, half)]
    phases = [[[[] for _ in range(2)] for _ in range(n)] for _ in events]
    kept = [[0, 0] for _ in range(n)]
    for col in range(n):
        me = place[col]

        def dist(c):
            ahead = (place[c] - me) % n
            return min(ahead, n - ahead)

        def token_id(c):
            ahead = (place[c] - me) % n
            if ahead == 0:
                return 0
            if ahead == half:
                return n - 1
            return 2 * ahead if ahead < half else 2 * (n - ahead) - 1

        for h in range(2):
            chunks = sorted(range(h * half, (h + 1) * half), key=lambda c: (dist(c), c))
            order[col, h] = [c - h * half for c in chunks]
            for row in range(2):
                for j, c in enumerate(chunks):
                    need = 0 if row == h else j + 1
                    piece = j if row == h else half + j
                    if dist(c) == half:
                        kept[col][row] = piece
                        continue
                    number = next(k for k, (d, r) in enumerate(events) if d >= dist(c) and r >= need)
                    phases[number][col][row].append((token_id(c), piece))
    return ring, order, events, phases, kept


def tie(values, after):
    values, after = tuple(values), tuple(after)
    return lax.optimization_barrier(values + after)[: len(values)]


def hbm(x):
    return pltpu.with_memory_space_constraint(x, pltpu.HBM)


def vmem(x):
    return pltpu.with_memory_space_constraint(x, pltpu.VMEM)


def merge(me, order, index, count, weight, values, piece, pieces):
    block = values.shape[1]
    blocks = weight.shape[0] // block // pieces
    width = weight.shape[1]
    col_blocks = width // block

    def kernel(me_ref, order_ref, index_ref, count_ref, w_ref, values_ref, out_ref, vbuf, wsem, vsem):
        first = order_ref[me_ref[0] * pieces + piece] * blocks
        value_copy = pltpu.make_async_copy(values_ref, vbuf, vsem)
        value_copy.start()

        def copy(k):
            rows = pl.ds(pl.multiple_of((first + k) * block, block), block)
            return pltpu.make_async_copy(w_ref.at[rows], out_ref.at[pl.ds(k * block, block)], wsem.at[k])

        for k in range(blocks):
            copy(k).start()
        value_copy.wait()
        for k in range(blocks):
            copy(k).wait()

        def slot(s, carry):
            which = index_ref[s]
            row = which // col_blocks
            row_here = row - first

            @pl.when(jnp.logical_and(row_here >= 0, row_here < blocks))
            def _():
                rows = pl.ds(pl.multiple_of(row_here * block, block), block)
                cols = pl.ds(pl.multiple_of((which - row * col_blocks) * block, block), block)
                value = vbuf[pl.ds(pl.multiple_of(s * block, block), block), :]
                old = out_ref[rows, cols]
                out_ref[rows, cols] = (old.astype(jnp.float32) + value.astype(jnp.float32)).astype(out_ref.dtype)

            return carry

        lax.fori_loop(0, count_ref[0], slot, 0)

    return pl.pallas_call(
        kernel,
        in_specs=[pl.BlockSpec(memory_space=pltpu.SMEM)] * 4 + [pl.BlockSpec(memory_space=pltpu.HBM)] * 2,
        out_specs=pl.BlockSpec(memory_space=pltpu.VMEM),
        out_shape=pltpu.VMEM((blocks * block, width), weight.dtype),
        scratch_shapes=[
            pltpu.VMEM(values.shape, values.dtype),
            pltpu.SemaphoreType.DMA((blocks,)),
            pltpu.SemaphoreType.DMA,
        ],
        compiler_params=pltpu.CompilerParams(vmem_limit_bytes=10 * 2**20),
        cost_estimate=pl.CostEstimate(flops=0, bytes_accessed=0, transcendentals=0),
        name=f"merge{piece}",
    )(me, order, index, count, hbm(weight), hbm(values))


def phase(me, table, tokens, pieces, spaces, acc, most, keep=None):
    rows, part = tokens[0][0].shape
    depth = part * STREAMS
    total = pieces[0].shape[1]
    width = 512 if total % 512 == 0 else 128
    tiles = total // width
    first = acc is None
    n_tokens, n_pieces = len(tokens), len(pieces)
    keep_pieces, keep_spaces = keep if keep else ([], [])
    n_keep = len(keep_pieces)

    def kernel(me_ref, table_ref, *refs):
        token_refs = refs[: n_tokens * STREAMS]
        refs = refs[n_tokens * STREAMS :]
        piece_refs, keep_refs, refs = refs[:n_pieces], refs[n_pieces : n_pieces + n_keep], refs[n_pieces + n_keep :]
        if not first:
            refs = refs[1:]
        out_ref, refs = refs[0], refs[1:]
        if keep:
            kept_ref, refs = refs[0], refs[1:]
        tbuf, wbuf, tsem, wsem, ksem = refs
        base = me_ref[0] * (2 + 2 * most)
        count = table_ref[base]

        def columns(tile):
            return pl.ds(pl.multiple_of(tile * width, width), width)

        def token_copy(ref, i, k):
            return pltpu.make_async_copy(ref, tbuf.at[i, :, pl.ds(k * part, part)], tsem.at[i, k])

        def piece_copy(ref, tile, slot):
            return pltpu.make_async_copy(ref.at[:, columns(tile)], wbuf.at[slot], wsem.at[slot])

        def start_piece(tile, i, slot):
            which = table_ref[base + 3 + 2 * i]
            for p in range(n_pieces):

                @pl.when(which == p)
                def _():
                    piece_copy(piece_refs[p], tile, slot).start()

        def following(tile, i, slot):
            wrap = i == count - 1
            slot = jnp.where(slot == W_SLOTS - 1, 0, slot + 1)
            return jnp.where(wrap, tile + 1, tile), jnp.where(wrap, 0, i + 1), slot

        @pl.when(count > 0)
        def _():
            ahead = (jnp.int32(0), jnp.int32(0), jnp.int32(0))
            for s in range(W_SLOTS - 1):
                start_piece(*ahead)
                ahead = following(*ahead)

                if s == 0:
                    for i in range(most):

                        @pl.when(i < count)
                        def _():
                            which = table_ref[base + 2 + 2 * i]
                            for t in range(n_tokens):

                                @pl.when(which == t)
                                def _():
                                    for k in range(STREAMS):
                                        token_copy(token_refs[t * STREAMS + k], i, k).start()

        if keep:
            which_kept = table_ref[base + 1]
            for p in range(n_keep):

                @pl.when(which_kept == p)
                def _():
                    pltpu.make_async_copy(keep_refs[p], kept_ref, ksem).start()

        @pl.when(count > 0)
        def _():
            def step_body(step, carry):
                tile, i, slot, ahead = carry

                @pl.when(ahead[0] < tiles)
                def _():
                    start_piece(*ahead)

                @pl.when(tile == 0)
                def _():
                    for k in range(STREAMS):
                        token_copy(token_refs[k], i, k).wait()

                piece_copy(piece_refs[0], tile, slot).wait()
                product = jnp.dot(tbuf[i], wbuf[slot], preferred_element_type=jnp.float32)
                if first:

                    @pl.when(i == 0)
                    def _():
                        out_ref[:, columns(tile)] = product

                    @pl.when(i > 0)
                    def _():
                        out_ref[:, columns(tile)] += product
                else:
                    out_ref[:, columns(tile)] += product
                return (*following(tile, i, slot), following(*ahead))

            zero = jnp.int32(0)
            ahead = (zero, zero, zero)
            for s in range(W_SLOTS - 1):
                ahead = following(*ahead)
            lax.fori_loop(0, count * tiles, step_body, (zero, zero, zero, ahead))

        if keep:
            pltpu.make_async_copy(keep_refs[0], kept_ref, ksem).wait()

    def specs(spaces):
        return [pl.BlockSpec(memory_space=space) for space in spaces]

    flat = [a for t in tokens for a in t]
    pin = {pl.ANY: lambda x: x, pltpu.HBM: hbm}
    pieces = [pin[space](p) for p, space in zip(pieces, spaces)]
    keep_pieces = [pin[space](p) for p, space in zip(keep_pieces, keep_spaces)]
    operands = [me, table] + flat + list(pieces) + list(keep_pieces) + ([] if first else [vmem(acc)])
    in_spaces = [pltpu.SMEM] * 2 + [pl.ANY] * len(flat) + list(spaces) + list(keep_spaces)
    in_spaces += [] if first else [pltpu.VMEM]
    out_shape = [pltpu.VMEM((rows, total), jnp.float32)]
    if keep:
        out_shape.append(pltpu.VMEM(pieces[0].shape, pieces[0].dtype))
    return pl.pallas_call(
        kernel,
        in_specs=specs(in_spaces),
        out_specs=specs([pltpu.VMEM] * len(out_shape)),
        out_shape=out_shape,
        scratch_shapes=[
            pltpu.VMEM((most, rows, depth), tokens[0][0].dtype),
            pltpu.VMEM((W_SLOTS, depth, width), pieces[0].dtype),
            pltpu.SemaphoreType.DMA((most, STREAMS)),
            pltpu.SemaphoreType.DMA((W_SLOTS,)),
            pltpu.SemaphoreType.DMA,
        ],
        input_output_aliases={} if first else {len(operands) - 1: 0},
        compiler_params=pltpu.CompilerParams(vmem_limit_bytes=12 * 2**20),
        cost_estimate=pl.CostEstimate(flops=0, bytes_accessed=0, transcendentals=0),
        name="phase",
    )(*operands)


def last_phase(tokens, weight, acc, out_dtype):
    rows, part = tokens[0].shape
    total = weight.shape[1]
    width = 512 if total % 512 == 0 else 128
    tiles = total // width
    n = len(tokens)

    def kernel(*refs):
        token_refs = refs[:n]
        w_ref, acc_ref, out_ref, obuf, osem = refs[n:]

        def store(tile):
            slot = lax.rem(tile, 2)
            at = pl.ds(pl.multiple_of(tile * width, width), width)
            return pltpu.make_async_copy(obuf.at[slot], out_ref.at[:, at], osem.at[slot])

        def step(tile, carry):
            at = pl.ds(pl.multiple_of(tile * width, width), width)
            total = acc_ref[:, at]
            for k in range(n):
                total = total + jnp.dot(
                    token_refs[k][...], w_ref[pl.ds(k * part, part), at], preferred_element_type=jnp.float32
                )

            @pl.when(tile >= 2)
            def _():
                store(tile - 2).wait()

            obuf[lax.rem(tile, 2)] = total.astype(out_dtype)
            store(tile).start()
            return carry

        lax.fori_loop(0, tiles, step, 0)
        for tile in range(max(0, tiles - 2), tiles):
            store(tile).wait()

    return pl.pallas_call(
        kernel,
        in_specs=[pl.BlockSpec(memory_space=pltpu.VMEM)] * (n + 2),
        out_specs=pl.BlockSpec(memory_space=pltpu.HBM),
        out_shape=jax.ShapeDtypeStruct((rows, total), out_dtype),
        scratch_shapes=[pltpu.VMEM((2, rows, width), out_dtype), pltpu.SemaphoreType.DMA((2,))],
        compiler_params=pltpu.CompilerParams(vmem_limit_bytes=24 * 2**20),
        cost_estimate=pl.CostEstimate(flops=0, bytes_accessed=0, transcendentals=0),
        name="last_phase",
    )(*tokens, vmem(weight), vmem(acc))


def body(tokens, base_weight, delta_values, delta_index, delta_count, n_col):
    ring, order, events, phases, kept = plan(n_col)
    half = n_col // 2
    ahead = [(ring[k], ring[(k + 1) % n_col]) for k in range(n_col)]
    behind = [(b, a) for a, b in ahead]
    swap = [(0, 1), (1, 0)]
    me = (lax.axis_index("col") * 2 + lax.axis_index("row")).astype(jnp.int32).reshape(1)
    index = delta_index.reshape(-1)
    count = delta_count.reshape(-1)
    order_table = jnp.asarray(order.reshape(-1))

    part = tokens.shape[1] // STREAMS
    own = [tokens[:, k * part : (k + 1) * part] for k in range(STREAMS)]
    buffers = [own]
    pieces = {}

    def step(d, k, fwd, bwd, after):
        fwd, bwd = tie((fwd, bwd), after)
        if d == half:
            return (lax.ppermute(fwd, "col", ahead),) * 2 if k < STREAMS // 2 else (lax.ppermute(bwd, "col", behind),) * 2
        return lax.ppermute(fwd, "col", ahead), lax.ppermute(bwd, "col", behind)

    def run(number, acc):
        lists = phases[number]
        most = max(1, max(len(lists[c][r]) for c in range(n_col) for r in range(2)))
        used_t = sorted({t for c in range(n_col) for r in range(2) for t, _ in lists[c][r]})
        used_p = sorted({p for c in range(n_col) for r in range(2) for _, p in lists[c][r]})
        final = number == len(events) - 1
        used_k = sorted({kept[c][r] for c in range(n_col) for r in range(2)}) if final else []
        table = np.zeros((n_col, 2, 2 + 2 * most), np.int32)
        for c in range(n_col):
            for r in range(2):
                table[c, r, 0] = len(lists[c][r])
                if final:
                    table[c, r, 1] = used_k.index(kept[c][r])
                for i, (t, p) in enumerate(lists[c][r]):
                    table[c, r, 2 + 2 * i] = used_t.index(t)
                    table[c, r, 3 + 2 * i] = used_p.index(p)

        def space(p):
            return pl.ANY if p < half else pltpu.HBM

        keep = ([pieces[p] for p in used_k], [space(p) for p in used_k]) if final else None
        return phase(
            me,
            jnp.asarray(table.reshape(-1)),
            [buffers[t] for t in used_t],
            [pieces[p] for p in used_p],
            [space(p) for p in used_p],
            acc,
            most,
            keep,
        )

    arrived = [step(1, k, own[k], own[k], ()) for k in range(STREAMS)]
    merged = []
    for j in range(half):
        merged.append(merge(me, order_table, index, count, base_weight, delta_values, j, half))
        pieces[j] = merged[j]
    pieces[half] = lax.ppermute(merged[0], "row", swap)

    acc = None
    sent = 1
    for d in range(1, half):
        for k in range(STREAMS):
            if sent < half:
                (piece,) = tie((merged[sent],), arrived[k])
                pieces[half + sent] = lax.ppermute(piece, "row", swap)
                sent += 1
        buffers += [[arrived[k][0] for k in range(STREAMS)], [arrived[k][1] for k in range(STREAMS)]]
        gates = [[acc]] * STREAMS if acc is not None else [[merged[half // 2]], [merged[half - 1]]]
        arrived = [step(d + 1, k, arrived[k][0], arrived[k][1], gates[k]) for k in range(STREAMS)]
        out = run(d - 1, acc)
        acc = out[0]
    return last_phase([arrived[k][0] for k in range(STREAMS)], out[1], acc, jnp.bfloat16)


def solution(mesh):
    spec = P(("tenant", "row"), "col")
    return jax.shard_map(
        functools.partial(body, n_col=mesh.shape["col"]),
        mesh=mesh,
        in_specs=(spec, P("row", "col"), spec, spec, spec),
        out_specs=spec,
        check_vma=False,
    )
```

```python
import functools

import jax
import jax.numpy as jnp
import numpy as np
from jax import lax
from jax.experimental import pallas as pl
from jax.experimental.pallas import tpu as pltpu
from jax.sharding import PartitionSpec as P

MERGE_VMEM = 10
PHASE_VMEM = 28


def ring_order(n):
    return list(range(0, n, 2)) + list(range(n - 1, 0, -2))


def plan(n):
    ring = ring_order(n)
    place = {c: k for k, c in enumerate(ring)}
    half = n // 2
    order = np.zeros((n, 2, half), np.int32)
    meets = np.zeros((n, 2, n), np.int32)
    for col in range(n):
        me = place[col]

        def dist(c):
            ahead = (place[c] - me) % n
            return min(ahead, n - ahead)

        def token_id(c):
            ahead = (place[c] - me) % n
            if ahead == 0:
                return 0
            if ahead == half:
                return n - 1
            return 2 * ahead if ahead < half else 2 * (n - ahead) - 1

        for h in range(2):
            chunks = sorted(range(h * half, (h + 1) * half), key=lambda c: (dist(c), c))
            order[col, h] = [c - h * half for c in chunks]
            for row in range(2):
                for j, c in enumerate(chunks):
                    meets[col, row, token_id(c)] = j if row == h else half + j
    return ring, order, meets.tolist()


def tie(values, after):
    n = len(values)

    def kernel(*refs):
        refs[-1][...] = jnp.zeros_like(refs[-1])

    return pl.pallas_call(
        kernel,
        in_specs=[pl.BlockSpec(memory_space=pl.ANY)] * (n + len(after)),
        out_specs=[pl.BlockSpec(memory_space=pl.ANY)] * n,
        out_shape=[jax.ShapeDtypeStruct(v.shape, v.dtype) for v in values],
        scratch_shapes=[pltpu.VMEM((8, 128), jnp.float32)],
        input_output_aliases={k: k for k in range(n)},
        compiler_params=pltpu.CompilerParams(vmem_limit_bytes=2**20),
        cost_estimate=pl.CostEstimate(flops=0, bytes_accessed=0, transcendentals=0),
        name="tie",
    )(*values, *after)


def hbm(x):
    return pltpu.with_memory_space_constraint(x, pltpu.HBM)


def merge(me, order, index, count, weight, values, piece, pieces, after=()):
    block = values.shape[1]
    blocks = weight.shape[0] // block // pieces
    width = weight.shape[1]
    col_blocks = width // block

    def kernel(me_ref, order_ref, index_ref, count_ref, w_ref, values_ref, *rest):
        out_ref, vbuf, wsem, vsem = rest[len(after) :]
        first = order_ref[me_ref[0] * pieces + piece] * blocks
        value_copy = pltpu.make_async_copy(values_ref, vbuf, vsem)
        value_copy.start()

        def copy(k):
            rows = pl.ds(pl.multiple_of((first + k) * block, block), block)
            return pltpu.make_async_copy(w_ref.at[rows], out_ref.at[pl.ds(k * block, block)], wsem.at[k])

        for k in range(blocks):
            copy(k).start()
        value_copy.wait()
        for k in range(blocks):
            copy(k).wait()

        def slot(s, carry):
            which = index_ref[s]
            row = which // col_blocks
            row_here = row - first

            @pl.when(jnp.logical_and(row_here >= 0, row_here < blocks))
            def _():
                rows = pl.ds(pl.multiple_of(row_here * block, block), block)
                cols = pl.ds(pl.multiple_of((which - row * col_blocks) * block, block), block)
                value = vbuf[pl.ds(pl.multiple_of(s * block, block), block), :]
                old = out_ref[rows, cols]
                out_ref[rows, cols] = (old.astype(jnp.float32) + value.astype(jnp.float32)).astype(out_ref.dtype)

            return carry

        lax.fori_loop(0, count_ref[0], slot, 0)

    return pl.pallas_call(
        kernel,
        in_specs=[pl.BlockSpec(memory_space=pltpu.SMEM)] * 4
        + [pl.BlockSpec(memory_space=pltpu.HBM)] * 2
        + [pl.BlockSpec(memory_space=pl.ANY)] * len(after),
        out_specs=pl.BlockSpec(memory_space=pltpu.VMEM),
        out_shape=pltpu.VMEM((blocks * block, width), weight.dtype),
        scratch_shapes=[
            pltpu.VMEM(values.shape, values.dtype),
            pltpu.SemaphoreType.DMA((blocks,)),
            pltpu.SemaphoreType.DMA,
        ],
        compiler_params=pltpu.CompilerParams(vmem_limit_bytes=MERGE_VMEM * 2**20),
        cost_estimate=pl.CostEstimate(flops=0, bytes_accessed=0, transcendentals=0),
        name=f"merge{piece}",
    )(me, order, index, count, hbm(weight), hbm(values), *after)


def tile_width(total):
    return 512 if total % 512 == 0 else total


def phase(me, table, counts, tokens, pieces, keep_pieces, accs, lo, hi):
    rows, depth = tokens[0].shape
    width = tile_width(pieces[0].shape[1])
    tiles = (hi - lo) // width
    n_tokens, n_pieces, n_keep, n_accs = len(tokens), len(pieces), len(keep_pieces), len(accs)
    starts = [0]
    for a in accs:
        starts.append(starts[-1] + a.shape[1] // width)
    most = max(counts)
    stride = 2 * most + 2

    def kernel(me_ref, table_ref, *refs):
        token_refs, refs = refs[:n_tokens], refs[n_tokens:]
        piece_refs, refs = refs[:n_pieces], refs[n_pieces:]
        keep_refs, refs = refs[:n_keep], refs[n_keep:]
        acc_refs, refs = refs[:n_accs], refs[n_accs:]
        out_ref, mark_ref, refs = refs[0], refs[1], refs[2:]
        if n_keep:
            kept_ref, refs = refs[0], refs[1:]
        tbuf, wbuf, abuf, tsem, wsem, asem, ksem = refs
        base = me_ref[0] * stride
        mark_ref[...] = jnp.zeros_like(mark_ref)

        def token_copy(ref, i):
            return pltpu.make_async_copy(ref, tbuf.at[:, pl.ds(i * depth, depth)], tsem.at[i])

        def piece_copy(ref, tile, i):
            slot = lax.rem(tile, 2)
            at = pl.ds(pl.multiple_of(lo + tile * width, 128), width)
            return pltpu.make_async_copy(ref.at[:, at], wbuf.at[slot, pl.ds(i * depth, depth)], wsem.at[slot, i])

        def acc_copy(ref, tile, start):
            slot = lax.rem(tile, 2)
            at = pl.ds(pl.multiple_of((tile - start) * width, 128), width)
            return pltpu.make_async_copy(ref.at[:, at], abuf.at[slot], asem.at[slot])

        def fetch(tile, count):
            for i in range(count):
                which = table_ref[base + 2 + 2 * i]
                for p in range(n_pieces):

                    @pl.when(which == p)
                    def _():
                        piece_copy(piece_refs[p], tile, i).start()

            for a in range(n_accs):

                @pl.when(jnp.logical_and(tile >= starts[a], tile < starts[a + 1]))
                def _():
                    acc_copy(acc_refs[a], tile, starts[a]).start()

        def work(count):
            for i in range(count):
                which = table_ref[base + 1 + 2 * i]
                for t in range(n_tokens):

                    @pl.when(which == t)
                    def _():
                        token_copy(token_refs[t], i).start()

            fetch(jnp.int32(0), count)
            for i in range(count):
                token_copy(token_refs[0], i).wait()

            def step(tile, carry):
                @pl.when(tile + 1 < tiles)
                def _():
                    fetch(tile + 1, count)

                slot = lax.rem(tile, 2)
                for i in range(count):
                    piece_copy(piece_refs[0], tile, i).wait()
                if n_accs:
                    acc_copy(acc_refs[0], tile, tile).wait()
                at = pl.ds(pl.multiple_of(tile * width, 128), width)
                deep = pl.ds(0, count * depth)
                product = jnp.dot(tbuf[:, deep], wbuf[slot, deep], preferred_element_type=jnp.float32)
                out_ref[:, at] = abuf[slot] + product if n_accs else product
                return carry

            lax.fori_loop(0, tiles, step, 0)

        if n_keep:
            which_kept = table_ref[base + stride - 1]
            for p in range(n_keep):

                @pl.when(which_kept == p)
                def _():
                    pltpu.make_async_copy(keep_refs[p], kept_ref, ksem).start()

        for count in counts:

            @pl.when(table_ref[base] == count)
            def _():
                work(count)

        if n_keep:
            pltpu.make_async_copy(keep_refs[0], kept_ref, ksem).wait()

    operands = [me, table] + list(tokens) + list(pieces) + list(keep_pieces) + list(accs)
    out_shape = [jax.ShapeDtypeStruct((rows, hi - lo), jnp.float32), jax.ShapeDtypeStruct((8, 128), jnp.float32)]
    if n_keep:
        out_shape.append(jax.ShapeDtypeStruct(pieces[0].shape, pieces[0].dtype))
    return pl.pallas_call(
        kernel,
        in_specs=[pl.BlockSpec(memory_space=pltpu.SMEM)] * 2 + [pl.BlockSpec(memory_space=pl.ANY)] * (len(operands) - 2),
        out_specs=[pl.BlockSpec(memory_space=pltpu.VMEM)] * len(out_shape),
        out_shape=out_shape,
        scratch_shapes=[
            pltpu.VMEM((rows, most * depth), tokens[0].dtype),
            pltpu.VMEM((2, most * depth, width), pieces[0].dtype),
            pltpu.VMEM((2, rows, width) if n_accs else (2, 8, 128), jnp.float32),
            pltpu.SemaphoreType.DMA((most,)),
            pltpu.SemaphoreType.DMA((2, most)),
            pltpu.SemaphoreType.DMA((2,)),
            pltpu.SemaphoreType.DMA,
        ],
        compiler_params=pltpu.CompilerParams(vmem_limit_bytes=PHASE_VMEM * 2**20),
        cost_estimate=pl.CostEstimate(flops=0, bytes_accessed=0, transcendentals=0),
        name="phase",
    )(*operands)


def last_phase(tokens, weight, acc, out_dtype):
    part, depth = tokens[0].shape
    rows = part * len(tokens)
    total = weight.shape[1]
    width = tile_width(total)
    tiles = total // width
    n = len(tokens)

    def kernel(*refs):
        token_refs = refs[:n]
        w_ref, acc_ref, out_ref, tbuf, obuf, tsem, osem = refs[n:]

        def store(tile):
            at = pl.ds(tile * width, width)
            return pltpu.make_async_copy(obuf.at[:, at], out_ref.at[:, at], osem.at[tile])

        copies = [
            pltpu.make_async_copy(token_refs[k], tbuf.at[pl.ds(k * part, part)], tsem.at[k]) for k in range(n)
        ]
        for copy in copies:
            copy.start()
        for copy in copies:
            copy.wait()
        for tile in range(tiles):
            at = pl.ds(tile * width, width)
            product = jnp.dot(tbuf[...], w_ref[:, at], preferred_element_type=jnp.float32)
            obuf[:, at] = (acc_ref[:, at] + product).astype(out_dtype)
            store(tile).start()
        for tile in range(tiles):
            store(tile).wait()

    return pl.pallas_call(
        kernel,
        in_specs=[pl.BlockSpec(memory_space=pl.ANY)] * n + [pl.BlockSpec(memory_space=pltpu.VMEM)] * 2,
        out_specs=pl.BlockSpec(memory_space=pltpu.HBM),
        out_shape=jax.ShapeDtypeStruct((rows, total), out_dtype),
        scratch_shapes=[
            pltpu.VMEM((rows, depth), tokens[0].dtype),
            pltpu.VMEM((rows, total), out_dtype),
            pltpu.SemaphoreType.DMA((n,)),
            pltpu.SemaphoreType.DMA((tiles,)),
        ],
        compiler_params=pltpu.CompilerParams(vmem_limit_bytes=28 * 2**20),
        cost_estimate=pl.CostEstimate(flops=0, bytes_accessed=0, transcendentals=0),
        name="last_phase",
    )(*tokens, weight, acc)


def body(tokens, base_weight, delta_values, delta_index, delta_count, n_col):
    ring, order, meets = plan(n_col)
    half = n_col // 2
    ahead = [(ring[k], ring[(k + 1) % n_col]) for k in range(n_col)]
    behind = [(b, a) for a, b in ahead]
    swap = [(0, 1), (1, 0)]
    me = (lax.axis_index("col") * 2 + lax.axis_index("row")).astype(jnp.int32).reshape(1)
    index = delta_index.reshape(-1)
    count = delta_count.reshape(-1)
    order_table = jnp.asarray(order.reshape(-1))

    buffers = [tokens]

    def run(want, accs, lo, hi, keep):
        lists = [[(t, p) for t, p in enumerate(row) if want(t, p)] for col in meets for row in col]
        counts = sorted({len(items) for items in lists})
        used_t = sorted({t for items in lists for t, _ in items})
        used_p = sorted({p for items in lists for _, p in items})
        last_pieces = [row[n_col - 1] for col in meets for row in col]
        used_k = sorted(set(last_pieces)) if keep else []
        table = np.zeros((len(lists), 2 * max(counts) + 2), np.int32)
        for k, items in enumerate(lists):
            table[k, 0] = len(items)
            for i, (t, p) in enumerate(items):
                table[k, 1 + 2 * i] = used_t.index(t)
                table[k, 2 + 2 * i] = used_p.index(p)
            if keep:
                table[k, -1] = used_k.index(last_pieces[k])
        return phase(
            me,
            jnp.asarray(table.reshape(-1)),
            counts,
            [buffers[t] for t in used_t],
            [pieces[p] for p in used_p],
            [pieces[p] for p in used_k],
            accs,
            lo,
            hi,
        )

    fwd, bwd = lax.ppermute(tokens, "col", ahead), lax.ppermute(tokens, "col", behind)
    local = [merge(me, order_table, index, count, base_weight, delta_values, j, half) for j in range(half)]
    remote = [lax.ppermute(piece, "row", swap) for piece in local[:-1]]
    late = n_col - 1

    total = base_weight.shape[1]
    width = tile_width(total)
    cut = -(-(total // width) // 2) * width
    cuts = [(0, cut), (cut, total)] if cut < total else [(0, total)]
    bounds = list(range(2, half - 1, 2)) + [half - 1]
    accs, start = [], 0
    gate = local[:-1]
    for d in range(2, half + 1):
        fwd, bwd = tie((fwd, bwd), gate)
        buffers += [fwd, bwd]
        if d == 3:
            (piece,) = tie((local[-1],), (fwd, bwd))
            remote.append(lax.ppermute(piece, "row", swap))
            pieces = local + remote
        if d < half:
            fwd, bwd = lax.ppermute(fwd, "col", ahead), lax.ppermute(bwd, "col", behind)
        else:
            part = tokens.shape[0] // 2
            fwd, bwd = lax.ppermute(fwd[:part], "col", ahead), lax.ppermute(bwd[part:], "col", behind)
        gate = []
        if d - 1 in bounds:
            stop = 2 * d - 1
            if d == half:
                acc, _, kept = run(lambda t, p: start <= t < stop or (t < start and p == late), accs, 0, total, True)
            else:
                outs = [
                    run(lambda t, p: start <= t < stop and p != late, accs[k : k + 1], lo, hi, False)
                    for k, (lo, hi) in enumerate(cuts)
                ]
                accs = [out[0] for out in outs]
                gate = [out[1] for out in outs]
            start = stop
    return last_phase([fwd, bwd], kept, acc, jnp.bfloat16)


def solution(mesh):
    spec = P(("tenant", "row"), "col")
    return jax.shard_map(
        functools.partial(body, n_col=mesh.shape["col"]),
        mesh=mesh,
        in_specs=(spec, P("row", "col"), spec, spec, spec),
        out_specs=spec,
        check_vma=False,
    )
```

```python
import functools

import jax
import jax.numpy as jnp
import numpy as np
from jax import lax
from jax.experimental import pallas as pl
from jax.experimental.pallas import tpu as pltpu
from jax.sharding import PartitionSpec as P

PHASE_VMEM = 30
SPARE = 64
PIN = 2


def ring_order(n):
    return list(range(0, n, 2)) + list(range(n - 1, 0, -2))


def plan(n):
    ring = ring_order(n)
    place = {c: k for k, c in enumerate(ring)}
    half = n // 2
    order = np.zeros((n, 2, half), np.int32)
    meets = np.zeros((n, 2, n), np.int32)
    for col in range(n):
        me = place[col]

        def dist(c):
            ahead = (place[c] - me) % n
            return min(ahead, n - ahead)

        def token_id(c):
            ahead = (place[c] - me) % n
            if ahead == 0:
                return 0
            if ahead == half:
                return n - 1
            return 2 * ahead if ahead < half else 2 * (n - ahead) - 1

        for h in range(2):
            chunks = sorted(range(h * half, (h + 1) * half), key=lambda c: (dist(c), c))
            order[col, h] = [c - h * half for c in chunks]
            for row in range(2):
                for j, c in enumerate(chunks):
                    meets[col, row, token_id(c)] = j if row == h else half + j
    return ring, order, meets.tolist()


def tie(values, after):
    n = len(values)

    def kernel(*refs):
        refs[-1][...] = jnp.zeros_like(refs[-1])

    return pl.pallas_call(
        kernel,
        in_specs=[pl.BlockSpec(memory_space=pl.ANY)] * (n + len(after)),
        out_specs=[pl.BlockSpec(memory_space=pl.ANY)] * n,
        out_shape=[jax.ShapeDtypeStruct(v.shape, v.dtype) for v in values],
        scratch_shapes=[pltpu.VMEM((8, 128), jnp.float32)],
        input_output_aliases={k: k for k in range(n)},
        compiler_params=pltpu.CompilerParams(vmem_limit_bytes=2**20),
        cost_estimate=pl.CostEstimate(flops=0, bytes_accessed=0, transcendentals=0),
        name="tie",
    )(*values, *after)


def hbm(x):
    return pltpu.with_memory_space_constraint(x, pltpu.HBM)


def merge(me, order, index, count, weight, values, numbers, total_pieces, spare):
    pieces = len(numbers)
    block = values.shape[1]
    blocks = weight.shape[0] // block // total_pieces
    width = weight.shape[1]
    col_blocks = width // block

    def kernel(me_ref, order_ref, index_ref, count_ref, w_ref, values_ref, out_ref, vbuf, wsem, vsem):
        value_copy = pltpu.make_async_copy(values_ref, vbuf, vsem)
        first = [order_ref[me_ref[0] * total_pieces + p] * blocks for p in numbers]

        def copy(k):
            rows = pl.ds(pl.multiple_of((first[k // blocks] + k % blocks) * block, block), block)
            return pltpu.make_async_copy(w_ref.at[rows], out_ref.at[pl.ds(k * block, block)], wsem.at[k])

        value_copy.start()
        for k in range(pieces * blocks):
            copy(k).start()
        if spare:
            rest = out_ref.at[pl.ds(pieces * blocks * block, spare)]
            rest[...] = jnp.zeros((spare, width), out_ref.dtype)
        value_copy.wait()
        for k in range(pieces * blocks):
            copy(k).wait()

        def slot(s, carry):
            which = index_ref[s]
            row = which // col_blocks
            for p in range(pieces):
                row_here = row - first[p]

                @pl.when(jnp.logical_and(row_here >= 0, row_here < blocks))
                def _():
                    rows = pl.ds(pl.multiple_of((p * blocks + row_here) * block, block), block)
                    cols = pl.ds(pl.multiple_of((which - row * col_blocks) * block, block), block)
                    value = vbuf[pl.ds(pl.multiple_of(s * block, block), block), :]
                    old = out_ref[rows, cols]
                    out_ref[rows, cols] = (old.astype(jnp.float32) + value.astype(jnp.float32)).astype(out_ref.dtype)

            return carry

        lax.fori_loop(0, count_ref[0], slot, 0)

    shape = (pieces * blocks * block + spare, width)
    held = 2 * (shape[0] * width + values.shape[0] * values.shape[1])
    return pl.pallas_call(
        kernel,
        in_specs=[pl.BlockSpec(memory_space=pltpu.SMEM)] * 4 + [pl.BlockSpec(memory_space=pltpu.HBM)] * 2,
        out_specs=pl.BlockSpec(memory_space=pltpu.VMEM),
        out_shape=pltpu.VMEM(shape, weight.dtype),
        scratch_shapes=[
            pltpu.VMEM(values.shape, values.dtype),
            pltpu.SemaphoreType.DMA((pieces * blocks,)),
            pltpu.SemaphoreType.DMA,
        ],
        compiler_params=pltpu.CompilerParams(vmem_limit_bytes=held + 2**20),
        cost_estimate=pl.CostEstimate(flops=0, bytes_accessed=0, transcendentals=0),
        name="merge",
    )(me, order, index, count, hbm(weight), hbm(values))


def tile_width(total):
    return 512 if total % 512 == 0 else total


def phase(me, table, kinds, tokens, weights, pinned, accs, last):
    n_tokens, n_weights, n_accs = len(tokens), len(weights), len(accs)
    rows, depth = tokens[0].shape
    total = weights[0].shape[1]
    width = tile_width(total)
    tiles = total // width
    most = max(max(count for count, _ in kinds), 1)
    stride = 4 + 3 * most
    slots = 3 if most > 3 else 4

    def kernel(me_ref, table_ref, *refs):
        token_refs, refs = refs[:n_tokens], refs[n_tokens:]
        weight_refs, refs = refs[:n_weights], refs[n_weights:]
        acc_refs, refs = refs[:n_accs], refs[n_accs:]
        out_ref, refs = refs[0], refs[1:]
        if last:
            kept_ref, refs = refs[0], refs[1:]
        tbuf, wbuf, abuf, obuf, tsem, wsem, asem, osem, ksem = refs
        base = me_ref[0] * stride

        def columns(tile):
            return pl.ds(pl.multiple_of(tile * width, 128), width)

        def token_copy(ref, i):
            return pltpu.make_async_copy(ref, tbuf.at[:, pl.ds(i * depth, depth)], tsem.at[i])

        def piece_rows(at):
            return pl.ds(pl.multiple_of(table_ref[at] * depth, depth), depth)

        def weight_copy(ref, tile, i):
            slot = lax.rem(tile, slots)
            return pltpu.make_async_copy(
                ref.at[piece_rows(base + 6 + 3 * i), columns(tile)], wbuf.at[slot, pl.ds(i * depth, depth)], wsem.at[slot, i]
            )

        def acc_copy(tile):
            slot = lax.rem(tile, slots)
            return pltpu.make_async_copy(acc_refs[0].at[:, columns(tile)], abuf.at[slot], asem.at[slot])

        def store(tile):
            slot = lax.rem(tile, 2)
            return pltpu.make_async_copy(obuf.at[slot], out_ref.at[:, columns(tile)], osem.at[slot])

        def fetch(tile, count, use_acc):
            for i in range(count):
                for w in range(n_weights):

                    @pl.when(table_ref[base + 5 + 3 * i] == w)
                    def _():
                        weight_copy(weight_refs[w], tile, i).start()

            if use_acc:
                acc_copy(tile).start()

        def work(count, use_acc):
            for i in range(count):
                for t in range(n_tokens):

                    @pl.when(table_ref[base + 4 + 3 * i] == t)
                    def _():
                        token_copy(token_refs[t], i).start()

            fetch(jnp.int32(0), count, use_acc)
            for i in range(count):
                token_copy(token_refs[0], i).wait()

            def step(tile, carry):
                if last:

                    @pl.when(tile == tiles // 2)
                    def _():
                        for w in range(n_weights):

                            @pl.when(table_ref[base + 2] == w)
                            def _():
                                pltpu.make_async_copy(weight_refs[w].at[piece_rows(base + 3)], kept_ref, ksem).start()

                slot = lax.rem(tile, slots)
                for i in range(count):
                    weight_copy(weight_refs[0], tile, i).wait()
                if use_acc:
                    acc_copy(tile).wait()

                @pl.when(tile == 0)
                def _():
                    for later in range(1, min(slots - 1, tiles)):
                        fetch(jnp.int32(later), count, use_acc)

                @pl.when(tile + slots - 1 < tiles)
                def _():
                    fetch(tile + slots - 1, count, use_acc)

                deep = pl.ds(0, count * depth)
                value = jnp.dot(tbuf[:, deep], wbuf[slot, deep], preferred_element_type=jnp.float32)
                if use_acc:
                    value = value + abuf[slot]
                if last:
                    out_ref[:, columns(tile)] = value
                else:

                    @pl.when(tile >= 2)
                    def _():
                        store(tile - 2).wait()

                    obuf[lax.rem(tile, 2)] = value
                    store(tile).start()
                return carry

            lax.fori_loop(0, tiles, step, 0)
            if last:
                pltpu.make_async_copy(weight_refs[0].at[pl.ds(0, depth)], kept_ref, ksem).wait()
            else:
                for tile in range(max(0, tiles - 2), tiles):
                    store(tile).wait()

        for count, use_acc in kinds:
            if count:

                @pl.when(jnp.logical_and(table_ref[base] == count, table_ref[base + 1] == use_acc))
                def _():
                    work(count, use_acc)

    place = pltpu.VMEM if last else pltpu.HBM
    out_shape = [place((rows, total), jnp.float32)]
    if last:
        out_shape.append(pltpu.VMEM((depth, total), weights[0].dtype))
    operands = [me, table] + list(tokens) + [hbm(w) if k in pinned else w for k, w in enumerate(weights)]
    operands += [hbm(a) for a in accs]
    return pl.pallas_call(
        kernel,
        in_specs=[pl.BlockSpec(memory_space=pltpu.SMEM)] * 2 + [pl.BlockSpec(memory_space=pl.ANY)] * (len(operands) - 2),
        out_specs=[pl.BlockSpec(memory_space=place)] * len(out_shape),
        out_shape=out_shape,
        scratch_shapes=[
            pltpu.VMEM((rows, most * depth), tokens[0].dtype),
            pltpu.VMEM((slots, most * depth, width), weights[0].dtype),
            pltpu.VMEM((slots, rows, width) if n_accs else (slots, 8, 128), jnp.float32),
            pltpu.VMEM((2, 8, 128) if last else (2, rows, width), jnp.float32),
            pltpu.SemaphoreType.DMA((most,)),
            pltpu.SemaphoreType.DMA((slots, most)),
            pltpu.SemaphoreType.DMA((slots,)),
            pltpu.SemaphoreType.DMA((2,)),
            pltpu.SemaphoreType.DMA,
        ],
        compiler_params=pltpu.CompilerParams(vmem_limit_bytes=PHASE_VMEM * 2**20),
        cost_estimate=pl.CostEstimate(flops=0, bytes_accessed=0, transcendentals=0),
        name="phase",
    )(*operands)


def last_phase(tokens, weight, acc, out_dtype):
    part, depth = tokens[0].shape
    rows = part * len(tokens)
    total = weight.shape[1]
    width = tile_width(total)
    tiles = total // width
    n = len(tokens)

    def kernel(*refs):
        token_refs = refs[:n]
        w_ref, acc_ref, out_ref, tbuf, obuf, tsem, osem = refs[n:]

        def store(tile):
            at = pl.ds(tile * width, width)
            return pltpu.make_async_copy(obuf.at[:, at], out_ref.at[:, at], osem.at[tile])

        copies = [
            pltpu.make_async_copy(token_refs[k], tbuf.at[pl.ds(k * part, part)], tsem.at[k]) for k in range(n)
        ]
        for copy in copies:
            copy.start()
        for copy in copies:
            copy.wait()
        for tile in range(tiles):
            at = pl.ds(tile * width, width)
            product = jnp.dot(tbuf[...], w_ref[:, at], preferred_element_type=jnp.float32)
            obuf[:, at] = (acc_ref[:, at] + product).astype(out_dtype)
            store(tile).start()
        for tile in range(tiles):
            store(tile).wait()

    return pl.pallas_call(
        kernel,
        in_specs=[pl.BlockSpec(memory_space=pl.ANY)] * n + [pl.BlockSpec(memory_space=pltpu.VMEM)] * 2,
        out_specs=pl.BlockSpec(memory_space=pltpu.HBM),
        out_shape=jax.ShapeDtypeStruct((rows, total), out_dtype),
        scratch_shapes=[
            pltpu.VMEM((rows, depth), tokens[0].dtype),
            pltpu.VMEM((rows, total), out_dtype),
            pltpu.SemaphoreType.DMA((n,)),
            pltpu.SemaphoreType.DMA((tiles,)),
        ],
        compiler_params=pltpu.CompilerParams(vmem_limit_bytes=28 * 2**20),
        cost_estimate=pl.CostEstimate(flops=0, bytes_accessed=0, transcendentals=0),
        name="last_phase",
    )(*tokens, weight, acc)


def body(tokens, base_weight, delta_values, delta_index, delta_count, n_col):
    ring, order, meets = plan(n_col)
    half = n_col // 2
    ahead = [(ring[k], ring[(k + 1) % n_col]) for k in range(n_col)]
    behind = [(b, a) for a, b in ahead]
    swap = [(0, 1), (1, 0)]
    me = (lax.axis_index("col") * 2 + lax.axis_index("row")).astype(jnp.int32).reshape(1)
    index = delta_index.reshape(-1)
    count = delta_count.reshape(-1)
    order_table = jnp.asarray(order.reshape(-1))
    devices = [row for col in meets for row in col]
    done = [set() for _ in devices]

    def run(want, acc, last):
        had = [bool(d) for d in done]
        lists = [
            [(t, p) for t, p in enumerate(row) if t not in d and want(t, p)] for row, d in zip(devices, done)
        ]
        kinds = sorted({(len(items), int(h)) for items, h in zip(lists, had)})
        used_t = sorted({t for items in lists for t, _ in items})
        ends = [row[n_col - 1] for row in devices] if last else []
        used_w = sorted({place[p][0] for items in lists for _, p in items} | {place[p][0] for p in ends})
        table = np.zeros((len(lists), 4 + 3 * max(max(k for k, _ in kinds), 1)), np.int32)
        for k, items in enumerate(lists):
            table[k, :2] = len(items), had[k]
            if last:
                table[k, 2:4] = used_w.index(place[ends[k]][0]), place[ends[k]][1]
            for i, (t, p) in enumerate(items):
                table[k, 4 + 3 * i : 7 + 3 * i] = used_t.index(t), used_w.index(place[p][0]), place[p][1]
                done[k].add(t)
        return phase(
            me,
            jnp.asarray(table.reshape(-1)),
            kinds,
            [buffers[t] for t in used_t],
            [weights[w] for w in used_w],
            [k for k, w in enumerate(used_w) if w < PIN],
            [] if acc is None else [acc],
            last,
        )

    fwd, bwd = lax.ppermute(tokens, "col", ahead), lax.ppermute(tokens, "col", behind)
    sets = [[0, half - 1], list(range(1, half - 1))]
    args = (me, order_table, index, count, base_weight, delta_values)
    local = [merge(*args, numbers, half, spare) for numbers, spare in zip(sets, (0, SPARE))]
    remote = [lax.ppermute(local[0], "row", swap), None]
    place = {}
    for w, numbers in enumerate(sets):
        for k, p in enumerate(numbers):
            place[p], place[half + p] = (w, k), (2 + w, k)
    buffers = [tokens]

    bounds = list(range(2, half - 1, 2)) + [half - 1]
    acc = None
    gate = list(local)
    for d in range(2, half + 1):
        fwd, bwd = tie((fwd, bwd), gate)
        buffers += [fwd, bwd]
        if d == 2:
            (local[1],) = tie((local[1],), (fwd, bwd))
            remote[1] = lax.ppermute(local[1], "row", swap)
            weights = local + remote
        if d < half:
            next_fwd, next_bwd = lax.ppermute(fwd, "col", ahead), lax.ppermute(bwd, "col", behind)
        else:
            part = tokens.shape[0] // 2
            next_fwd, next_bwd = lax.ppermute(fwd[:part], "col", ahead), lax.ppermute(bwd[part:], "col", behind)
        gate = []
        if d == 2:
            weights = local + remote
            acc = run(lambda t, p: t == 0, None, False)[0]
            gate = [hbm(acc)]
        elif d - 1 in bounds:
            out = run(lambda t, p: t < 2 * d - 1, acc, d == half)
            acc, gate = out[0], [hbm(out[0])]
        fwd, bwd = next_fwd, next_bwd
    return last_phase([fwd, bwd], out[1], acc, jnp.bfloat16)


def solution(mesh):
    spec = P(("tenant", "row"), "col")
    return jax.shard_map(
        functools.partial(body, n_col=mesh.shape["col"]),
        mesh=mesh,
        in_specs=(spec, P("row", "col"), spec, spec, spec),
        out_specs=spec,
        check_vma=False,
    )
```

```python
import functools

import jax
import jax.numpy as jnp
import numpy as np
from jax import lax
from jax.experimental import pallas as pl
from jax.experimental.pallas import tpu as pltpu
from jax.sharding import PartitionSpec as P

PHASE_VMEM = 26
SPARE = 64
PIN = 4


def ring_order(n):
    return list(range(0, n, 2)) + list(range(n - 1, 0, -2))


def plan(n):
    ring = ring_order(n)
    place = {c: k for k, c in enumerate(ring)}
    half = n // 2
    order = np.zeros((n, 2, half), np.int32)
    meets = np.zeros((n, 2, n), np.int32)
    for col in range(n):
        me = place[col]

        def dist(c):
            ahead = (place[c] - me) % n
            return min(ahead, n - ahead)

        def token_id(c):
            ahead = (place[c] - me) % n
            if ahead == 0:
                return 0
            if ahead == half:
                return n - 1
            return 2 * ahead if ahead < half else 2 * (n - ahead) - 1

        for h in range(2):
            chunks = sorted(range(h * half, (h + 1) * half), key=lambda c: (dist(c), c))
            order[col, h] = [c - h * half for c in chunks]
            for row in range(2):
                for j, c in enumerate(chunks):
                    meets[col, row, token_id(c)] = j if row == h else half + j
    return ring, order, meets.tolist()


def tie(values, after):
    n = len(values)

    def kernel(*refs):
        refs[-1][...] = jnp.zeros_like(refs[-1])

    return pl.pallas_call(
        kernel,
        in_specs=[pl.BlockSpec(memory_space=pl.ANY)] * (n + len(after)),
        out_specs=[pl.BlockSpec(memory_space=pl.ANY)] * n,
        out_shape=[jax.ShapeDtypeStruct(v.shape, v.dtype) for v in values],
        scratch_shapes=[pltpu.VMEM((8, 128), jnp.float32)],
        input_output_aliases={k: k for k in range(n)},
        compiler_params=pltpu.CompilerParams(vmem_limit_bytes=2**20),
        cost_estimate=pl.CostEstimate(flops=0, bytes_accessed=0, transcendentals=0),
        name="tie",
    )(*values, *after)


def hbm(x):
    return pltpu.with_memory_space_constraint(x, pltpu.HBM)


def merge(me, order, index, count, weight, values, numbers, total_pieces, spare):
    pieces = len(numbers)
    block = values.shape[1]
    blocks = weight.shape[0] // block // total_pieces
    width = weight.shape[1]
    col_blocks = width // block

    def kernel(me_ref, order_ref, index_ref, count_ref, w_ref, values_ref, out_ref, vbuf, wsem, vsem):
        value_copy = pltpu.make_async_copy(values_ref, vbuf, vsem)
        first = [order_ref[me_ref[0] * total_pieces + p] * blocks for p in numbers]

        def copy(k):
            rows = pl.ds(pl.multiple_of((first[k // blocks] + k % blocks) * block, block), block)
            return pltpu.make_async_copy(w_ref.at[rows], out_ref.at[pl.ds(k * block, block)], wsem.at[k])

        value_copy.start()
        for k in range(pieces * blocks):
            copy(k).start()
        if spare:
            rest = out_ref.at[pl.ds(pieces * blocks * block, spare)]
            rest[...] = jnp.zeros((spare, width), out_ref.dtype)
        value_copy.wait()
        for k in range(pieces * blocks):
            copy(k).wait()

        def slot(s, carry):
            which = index_ref[s]
            row = which // col_blocks
            for p in range(pieces):
                row_here = row - first[p]

                @pl.when(jnp.logical_and(row_here >= 0, row_here < blocks))
                def _():
                    rows = pl.ds(pl.multiple_of((p * blocks + row_here) * block, block), block)
                    cols = pl.ds(pl.multiple_of((which - row * col_blocks) * block, block), block)
                    value = vbuf[pl.ds(pl.multiple_of(s * block, block), block), :]
                    old = out_ref[rows, cols]
                    out_ref[rows, cols] = (old.astype(jnp.float32) + value.astype(jnp.float32)).astype(out_ref.dtype)

            return carry

        lax.fori_loop(0, count_ref[0], slot, 0)

    shape = (pieces * blocks * block + spare, width)
    held = 2 * (shape[0] * width + values.shape[0] * values.shape[1])
    return pl.pallas_call(
        kernel,
        in_specs=[pl.BlockSpec(memory_space=pltpu.SMEM)] * 4 + [pl.BlockSpec(memory_space=pltpu.HBM)] * 2,
        out_specs=pl.BlockSpec(memory_space=pltpu.VMEM),
        out_shape=pltpu.VMEM(shape, weight.dtype),
        scratch_shapes=[
            pltpu.VMEM(values.shape, values.dtype),
            pltpu.SemaphoreType.DMA((pieces * blocks,)),
            pltpu.SemaphoreType.DMA,
        ],
        compiler_params=pltpu.CompilerParams(vmem_limit_bytes=held + 2**20),
        cost_estimate=pl.CostEstimate(flops=0, bytes_accessed=0, transcendentals=0),
        name="merge",
    )(me, order, index, count, hbm(weight), hbm(values))


def tile_width(total):
    return 512 if total % 512 == 0 else total


def phase(me, table, kinds, tokens, weights, pinned, accs, last, keep):
    n_tokens, n_weights, n_accs = len(tokens), len(weights), len(accs)
    rows, depth = tokens[0].shape
    total = weights[0].shape[1]
    width = tile_width(total)
    tiles = total // width
    most = max(max(count for count, _ in kinds), 1)
    stride = 4 + 3 * most
    slots = 3 if most > 3 else 4

    def kernel(me_ref, table_ref, *refs):
        token_refs, refs = refs[:n_tokens], refs[n_tokens:]
        weight_refs, refs = refs[:n_weights], refs[n_weights:]
        acc_refs, refs = refs[:n_accs], refs[n_accs:]
        out_ref, refs = refs[0], refs[1:]
        if keep:
            kept_ref, refs = refs[0], refs[1:]
        tbuf, wbuf, abuf, obuf, tsem, wsem, asem, osem, ksem = refs
        base = me_ref[0] * stride

        def columns(tile):
            return pl.ds(pl.multiple_of(tile * width, 128), width)

        def token_copy(ref, i):
            return pltpu.make_async_copy(ref, tbuf.at[:, pl.ds(i * depth, depth)], tsem.at[i])

        def piece_rows(at):
            return pl.ds(pl.multiple_of(table_ref[at] * depth, depth), depth)

        def weight_copy(ref, tile, i):
            slot = lax.rem(tile, slots)
            return pltpu.make_async_copy(
                ref.at[piece_rows(base + 6 + 3 * i), columns(tile)], wbuf.at[slot, pl.ds(i * depth, depth)], wsem.at[slot, i]
            )

        def acc_copy(tile):
            slot = lax.rem(tile, slots)
            return pltpu.make_async_copy(acc_refs[0].at[:, columns(tile)], abuf.at[slot], asem.at[slot])

        def store(tile):
            slot = lax.rem(tile, 2)
            return pltpu.make_async_copy(obuf.at[slot], out_ref.at[:, columns(tile)], osem.at[slot])

        def fetch(tile, count, use_acc):
            for i in range(count):
                for w in range(n_weights):

                    @pl.when(table_ref[base + 5 + 3 * i] == w)
                    def _():
                        weight_copy(weight_refs[w], tile, i).start()

            if use_acc:
                acc_copy(tile).start()

        def work(count, use_acc):
            for i in range(count):
                for t in range(n_tokens):

                    @pl.when(table_ref[base + 4 + 3 * i] == t)
                    def _():
                        token_copy(token_refs[t], i).start()

            fetch(jnp.int32(0), count, use_acc)
            for i in range(count):
                token_copy(token_refs[0], i).wait()

            def step(tile, carry):
                if keep:

                    @pl.when(tile == tiles // 2)
                    def _():
                        for w in range(n_weights):

                            @pl.when(table_ref[base + 2] == w)
                            def _():
                                pltpu.make_async_copy(weight_refs[w].at[piece_rows(base + 3)], kept_ref, ksem).start()

                slot = lax.rem(tile, slots)
                for i in range(count):
                    weight_copy(weight_refs[0], tile, i).wait()
                if use_acc:
                    acc_copy(tile).wait()

                @pl.when(tile == 0)
                def _():
                    for later in range(1, min(slots - 1, tiles)):
                        fetch(jnp.int32(later), count, use_acc)

                @pl.when(tile + slots - 1 < tiles)
                def _():
                    fetch(tile + slots - 1, count, use_acc)

                deep = pl.ds(0, count * depth)
                value = jnp.dot(tbuf[:, deep], wbuf[slot, deep], preferred_element_type=jnp.float32)
                if use_acc:
                    value = value + abuf[slot]
                if last:
                    out_ref[:, columns(tile)] = value
                else:

                    @pl.when(tile >= 2)
                    def _():
                        store(tile - 2).wait()

                    obuf[lax.rem(tile, 2)] = value
                    store(tile).start()
                return carry

            lax.fori_loop(0, tiles, step, 0)
            if keep:
                pltpu.make_async_copy(weight_refs[0].at[pl.ds(0, depth)], kept_ref, ksem).wait()
            if not last:
                for tile in range(max(0, tiles - 2), tiles):
                    store(tile).wait()

        for count, use_acc in kinds:
            if count:

                @pl.when(jnp.logical_and(table_ref[base] == count, table_ref[base + 1] == use_acc))
                def _():
                    work(count, use_acc)

    place = pltpu.VMEM if last else pltpu.HBM
    out_shape = [place((rows, total), jnp.float32)]
    out_spaces = [place]
    if keep:
        out_shape.append(pltpu.VMEM((depth, total), weights[0].dtype))
        out_spaces.append(pltpu.VMEM)
    operands = [me, table] + list(tokens) + [hbm(w) if k in pinned else w for k, w in enumerate(weights)]
    operands += [hbm(a) for a in accs]
    return pl.pallas_call(
        kernel,
        in_specs=[pl.BlockSpec(memory_space=pltpu.SMEM)] * 2 + [pl.BlockSpec(memory_space=pl.ANY)] * (len(operands) - 2),
        out_specs=[pl.BlockSpec(memory_space=space) for space in out_spaces],
        out_shape=out_shape,
        scratch_shapes=[
            pltpu.VMEM((rows, most * depth), tokens[0].dtype),
            pltpu.VMEM((slots, most * depth, width), weights[0].dtype),
            pltpu.VMEM((slots, rows, width) if n_accs else (slots, 8, 128), jnp.float32),
            pltpu.VMEM((2, 8, 128) if last else (2, rows, width), jnp.float32),
            pltpu.SemaphoreType.DMA((most,)),
            pltpu.SemaphoreType.DMA((slots, most)),
            pltpu.SemaphoreType.DMA((slots,)),
            pltpu.SemaphoreType.DMA((2,)),
            pltpu.SemaphoreType.DMA,
        ],
        compiler_params=pltpu.CompilerParams(vmem_limit_bytes=PHASE_VMEM * 2**20),
        cost_estimate=pl.CostEstimate(flops=0, bytes_accessed=0, transcendentals=0),
        name="phase",
    )(*operands)


def last_phase(tokens, weight, acc, out_dtype):
    part, depth = tokens[0].shape
    rows = part * len(tokens)
    total = weight.shape[1]
    width = tile_width(total)
    tiles = total // width
    n = len(tokens)

    def kernel(*refs):
        token_refs = refs[:n]
        w_ref, acc_ref, out_ref, tbuf, obuf, tsem, osem = refs[n:]

        def store(tile):
            at = pl.ds(tile * width, width)
            return pltpu.make_async_copy(obuf.at[:, at], out_ref.at[:, at], osem.at[tile])

        copies = [
            pltpu.make_async_copy(token_refs[k], tbuf.at[pl.ds(k * part, part)], tsem.at[k]) for k in range(n)
        ]
        for copy in copies:
            copy.start()
        for copy in copies:
            copy.wait()
        for tile in range(tiles):
            at = pl.ds(tile * width, width)
            product = jnp.dot(tbuf[...], w_ref[:, at], preferred_element_type=jnp.float32)
            obuf[:, at] = (acc_ref[:, at] + product).astype(out_dtype)
            store(tile).start()
        for tile in range(tiles):
            store(tile).wait()

    return pl.pallas_call(
        kernel,
        in_specs=[pl.BlockSpec(memory_space=pl.ANY)] * n + [pl.BlockSpec(memory_space=pltpu.VMEM)] * 2,
        out_specs=pl.BlockSpec(memory_space=pltpu.HBM),
        out_shape=jax.ShapeDtypeStruct((rows, total), out_dtype),
        scratch_shapes=[
            pltpu.VMEM((rows, depth), tokens[0].dtype),
            pltpu.VMEM((rows, total), out_dtype),
            pltpu.SemaphoreType.DMA((n,)),
            pltpu.SemaphoreType.DMA((tiles,)),
        ],
        compiler_params=pltpu.CompilerParams(vmem_limit_bytes=28 * 2**20),
        cost_estimate=pl.CostEstimate(flops=0, bytes_accessed=0, transcendentals=0),
        name="last_phase",
    )(*tokens, weight, acc)


def body(tokens, base_weight, delta_values, delta_index, delta_count, n_col):
    ring, order, meets = plan(n_col)
    half = n_col // 2
    ahead = [(ring[k], ring[(k + 1) % n_col]) for k in range(n_col)]
    behind = [(b, a) for a, b in ahead]
    swap = [(0, 1), (1, 0)]
    me = (lax.axis_index("col") * 2 + lax.axis_index("row")).astype(jnp.int32).reshape(1)
    index = delta_index.reshape(-1)
    count = delta_count.reshape(-1)
    order_table = jnp.asarray(order.reshape(-1))
    devices = [row for col in meets for row in col]
    done = [set() for _ in devices]

    def run(want, acc, last, keep):
        had = [bool(d) for d in done]
        lists = [
            [(t, p) for t, p in enumerate(row) if t not in d and want(t, p)] for row, d in zip(devices, done)
        ]
        kinds = sorted({(len(items), int(h)) for items, h in zip(lists, had)})
        used_t = sorted({t for items in lists for t, _ in items})
        ends = [row[n_col - 1] for row in devices] if keep else []
        used_w = sorted({place[p][0] for items in lists for _, p in items} | {place[p][0] for p in ends})
        table = np.zeros((len(lists), 4 + 3 * max(max(k for k, _ in kinds), 1)), np.int32)
        for k, items in enumerate(lists):
            table[k, :2] = len(items), had[k]
            if keep:
                table[k, 2:4] = used_w.index(place[ends[k]][0]), place[ends[k]][1]
            for i, (t, p) in enumerate(items):
                table[k, 4 + 3 * i : 7 + 3 * i] = used_t.index(t), used_w.index(place[p][0]), place[p][1]
                done[k].add(t)
        return phase(
            me,
            jnp.asarray(table.reshape(-1)),
            kinds,
            [buffers[t] for t in used_t],
            [weights[w] for w in used_w],
            [k for k, w in enumerate(used_w) if w < PIN],
            [] if acc is None else [acc],
            last,
            keep,
        )

    fwd, bwd = lax.ppermute(tokens, "col", ahead), lax.ppermute(tokens, "col", behind)
    sets = [[0, half - 1], list(range(1, half - 1))]
    args = (me, order_table, index, count, base_weight, delta_values)
    local = [merge(*args, numbers, half, spare) for numbers, spare in zip(sets, (0, SPARE))]
    remote = [lax.ppermute(local[0], "row", swap), None]
    place = {}
    for w, numbers in enumerate(sets):
        for k, p in enumerate(numbers):
            place[p], place[half + p] = (w, k), (2 + w, k)
    buffers = [tokens]

    bounds = list(range(2, half - 1, 2)) + [half - 1]
    acc = None
    gate = list(local)
    for d in range(2, half + 1):
        (fwd,), (bwd,) = tie((fwd,), gate), tie((bwd,), gate)
        buffers += [fwd, bwd]
        if d == 2:
            (local[1],) = tie((local[1],), (fwd, bwd))
            remote[1] = lax.ppermute(local[1], "row", swap)
            weights = local + remote
        if d < half:
            next_fwd, next_bwd = lax.ppermute(fwd, "col", ahead), lax.ppermute(bwd, "col", behind)
        else:
            part = tokens.shape[0] // 2
            next_fwd, next_bwd = lax.ppermute(fwd[:part], "col", ahead), lax.ppermute(bwd[part:], "col", behind)
        gate = []
        if d == 2:
            weights = local + remote
            acc, kept = run(lambda t, p: t == 0, None, False, True)
            gate = [hbm(acc)]
        elif d - 1 in bounds:
            (acc,) = run(lambda t, p: t < 2 * d - 1, acc, d == half, False)
            gate = [hbm(acc)]
        fwd, bwd = next_fwd, next_bwd
    return last_phase([fwd, bwd], kept, acc, jnp.bfloat16)


def solution(mesh):
    spec = P(("tenant", "row"), "col")
    return jax.shard_map(
        functools.partial(body, n_col=mesh.shape["col"]),
        mesh=mesh,
        in_specs=(spec, P("row", "col"), spec, spec, spec),
        out_specs=spec,
        check_vma=False,
    )
```

```python
import functools

import jax
import jax.numpy as jnp
import numpy as np
from jax import lax
from jax.experimental import pallas as pl
from jax.experimental.pallas import tpu as pltpu
from jax.sharding import PartitionSpec as P

PHASE_VMEM = 26
SPARE = 16
PIN = 4


def ring_order(n):
    return list(range(0, n, 2)) + list(range(n - 1, 0, -2))


def plan(n):
    ring = ring_order(n)
    place = {c: k for k, c in enumerate(ring)}
    half = n // 2
    order = np.zeros((n, 2, half), np.int32)
    meets = np.zeros((n, 2, n), np.int32)
    for col in range(n):
        me = place[col]

        def dist(c):
            ahead = (place[c] - me) % n
            return min(ahead, n - ahead)

        def token_id(c):
            ahead = (place[c] - me) % n
            if ahead == 0:
                return 0
            if ahead == half:
                return n - 1
            return 2 * ahead if ahead < half else 2 * (n - ahead) - 1

        for h in range(2):
            chunks = sorted(range(h * half, (h + 1) * half), key=lambda c: (dist(c), c))
            order[col, h] = [c - h * half for c in chunks]
            for row in range(2):
                for j, c in enumerate(chunks):
                    meets[col, row, token_id(c)] = j if row == h else half + j
    return ring, order, meets.tolist()


def tie(values, after):
    n = len(values)

    def kernel(*refs):
        refs[-1][...] = jnp.zeros_like(refs[-1])

    return pl.pallas_call(
        kernel,
        in_specs=[pl.BlockSpec(memory_space=pl.ANY)] * (n + len(after)),
        out_specs=[pl.BlockSpec(memory_space=pl.ANY)] * n,
        out_shape=[jax.ShapeDtypeStruct(v.shape, v.dtype) for v in values],
        scratch_shapes=[pltpu.VMEM((8, 128), jnp.float32)],
        input_output_aliases={k: k for k in range(n)},
        compiler_params=pltpu.CompilerParams(vmem_limit_bytes=2**20),
        cost_estimate=pl.CostEstimate(flops=0, bytes_accessed=0, transcendentals=0),
        name="tie",
    )(*values, *after)


def hbm(x):
    return pltpu.with_memory_space_constraint(x, pltpu.HBM)


def merge(me, order, index, count, weight, values, numbers, total_pieces, spare):
    pieces = len(numbers)
    block = values.shape[1]
    blocks = weight.shape[0] // block // total_pieces
    width = weight.shape[1]
    col_blocks = width // block

    def kernel(me_ref, index_ref, count_ref, w_ref, values_ref, out_ref, vbuf, wsem, vsem):
        def chunk(p):
            found = jnp.int32(0)
            for k, chunks in enumerate(order):
                found = jnp.where(me_ref[0] == k, int(chunks[p]), found)
            return found

        value_copy = pltpu.make_async_copy(values_ref, vbuf, vsem)
        first = [chunk(p) * blocks for p in numbers]

        def copy(k):
            rows = pl.ds(pl.multiple_of((first[k // blocks] + k % blocks) * block, block), block)
            return pltpu.make_async_copy(w_ref.at[rows], out_ref.at[pl.ds(k * block, block)], wsem.at[k])

        value_copy.start()
        for k in range(pieces * blocks):
            copy(k).start()
        if spare:
            rest = out_ref.at[pl.ds(pieces * blocks * block, spare)]
            rest[...] = jnp.zeros((spare, width), out_ref.dtype)
        value_copy.wait()
        for k in range(pieces * blocks):
            copy(k).wait()

        def slot(s, carry):
            which = index_ref[s]
            row = which // col_blocks
            for p in range(pieces):
                row_here = row - first[p]

                @pl.when(jnp.logical_and(row_here >= 0, row_here < blocks))
                def _():
                    rows = pl.ds(pl.multiple_of((p * blocks + row_here) * block, block), block)
                    cols = pl.ds(pl.multiple_of((which - row * col_blocks) * block, block), block)
                    value = vbuf[pl.ds(pl.multiple_of(s * block, block), block), :]
                    old = out_ref[rows, cols]
                    out_ref[rows, cols] = (old.astype(jnp.float32) + value.astype(jnp.float32)).astype(out_ref.dtype)

            return carry

        lax.fori_loop(0, count_ref[0], slot, 0)

    shape = (pieces * blocks * block + spare, width)
    held = 2 * (shape[0] * width + values.shape[0] * values.shape[1])
    return pl.pallas_call(
        kernel,
        in_specs=[pl.BlockSpec(memory_space=pltpu.SMEM)] * 3 + [pl.BlockSpec(memory_space=pltpu.HBM)] * 2,
        out_specs=pl.BlockSpec(memory_space=pltpu.VMEM),
        out_shape=pltpu.VMEM(shape, weight.dtype),
        scratch_shapes=[
            pltpu.VMEM(values.shape, values.dtype),
            pltpu.SemaphoreType.DMA((pieces * blocks,)),
            pltpu.SemaphoreType.DMA,
        ],
        compiler_params=pltpu.CompilerParams(vmem_limit_bytes=held + 2**20),
        cost_estimate=pl.CostEstimate(flops=0, bytes_accessed=0, transcendentals=0),
        name="merge",
    )(me, index, count, hbm(weight), hbm(values))


def tile_width(total):
    return 512 if total % 512 == 0 else total


def phase(me, table, kinds, tokens, weights, pinned, accs, last, keep):
    n_tokens, n_weights, n_accs = len(tokens), len(weights), len(accs)
    rows, depth = tokens[0].shape
    total = weights[0].shape[1]
    width = tile_width(total)
    tiles = total // width
    most = max(max(count for count, _ in kinds), 1)
    stride = 4 + 3 * most
    slots = 3 if most > 3 else 4

    def kernel(me_ref, table_ref, *refs):
        token_refs, refs = refs[:n_tokens], refs[n_tokens:]
        weight_refs, refs = refs[:n_weights], refs[n_weights:]
        acc_refs, refs = refs[:n_accs], refs[n_accs:]
        out_ref, refs = refs[0], refs[1:]
        if keep:
            kept_ref, refs = refs[0], refs[1:]
        tbuf, wbuf, abuf, obuf, tsem, wsem, asem, osem, ksem = refs
        base = me_ref[0] * stride

        def columns(tile):
            return pl.ds(pl.multiple_of(tile * width, 128), width)

        def token_copy(ref, i):
            return pltpu.make_async_copy(ref, tbuf.at[:, pl.ds(i * depth, depth)], tsem.at[i])

        def piece_rows(at):
            return pl.ds(pl.multiple_of(table_ref[at] * depth, depth), depth)

        def weight_copy(ref, tile, i):
            slot = lax.rem(tile, slots)
            return pltpu.make_async_copy(
                ref.at[piece_rows(base + 6 + 3 * i), columns(tile)], wbuf.at[slot, pl.ds(i * depth, depth)], wsem.at[slot, i]
            )

        def acc_copy(tile):
            slot = lax.rem(tile, slots)
            return pltpu.make_async_copy(acc_refs[0].at[:, columns(tile)], abuf.at[slot], asem.at[slot])

        def store(tile):
            slot = lax.rem(tile, 2)
            return pltpu.make_async_copy(obuf.at[slot], out_ref.at[:, columns(tile)], osem.at[slot])

        def fetch(tile, count, use_acc):
            for i in range(count):
                for w in range(n_weights):

                    @pl.when(table_ref[base + 5 + 3 * i] == w)
                    def _():
                        weight_copy(weight_refs[w], tile, i).start()

            if use_acc:
                acc_copy(tile).start()

        def work(count, use_acc):
            for i in range(count):
                for t in range(n_tokens):

                    @pl.when(table_ref[base + 4 + 3 * i] == t)
                    def _():
                        token_copy(token_refs[t], i).start()

            fetch(jnp.int32(0), count, use_acc)
            for i in range(count):
                token_copy(token_refs[0], i).wait()

            def step(tile, carry):
                if keep:

                    @pl.when(tile == tiles // 2)
                    def _():
                        for w in range(n_weights):

                            @pl.when(table_ref[base + 2] == w)
                            def _():
                                pltpu.make_async_copy(weight_refs[w].at[piece_rows(base + 3)], kept_ref, ksem).start()

                slot = lax.rem(tile, slots)
                for i in range(count):
                    weight_copy(weight_refs[0], tile, i).wait()
                if use_acc:
                    acc_copy(tile).wait()

                @pl.when(tile == 0)
                def _():
                    for later in range(1, min(slots - 1, tiles)):
                        fetch(jnp.int32(later), count, use_acc)

                @pl.when(tile + slots - 1 < tiles)
                def _():
                    fetch(tile + slots - 1, count, use_acc)

                deep = pl.ds(0, count * depth)
                value = jnp.dot(tbuf[:, deep], wbuf[slot, deep], preferred_element_type=jnp.float32)
                if use_acc:
                    value = value + abuf[slot]
                if last:
                    out_ref[:, columns(tile)] = value
                else:

                    @pl.when(tile >= 2)
                    def _():
                        store(tile - 2).wait()

                    obuf[lax.rem(tile, 2)] = value
                    store(tile).start()
                return carry

            lax.fori_loop(0, tiles, step, 0)
            if keep:
                pltpu.make_async_copy(weight_refs[0].at[pl.ds(0, depth)], kept_ref, ksem).wait()
            if not last:
                for tile in range(max(0, tiles - 2), tiles):
                    store(tile).wait()

        for count, use_acc in kinds:
            if count:

                @pl.when(jnp.logical_and(table_ref[base] == count, table_ref[base + 1] == use_acc))
                def _():
                    work(count, use_acc)

    place = pltpu.VMEM if last else pltpu.HBM
    out_shape = [place((rows, total), jnp.float32)]
    out_spaces = [place]
    if keep:
        out_shape.append(pltpu.VMEM((depth, total), weights[0].dtype))
        out_spaces.append(pltpu.VMEM)
    operands = [me, table] + list(tokens) + [hbm(w) if k in pinned else w for k, w in enumerate(weights)]
    operands += [hbm(a) for a in accs]
    return pl.pallas_call(
        kernel,
        in_specs=[pl.BlockSpec(memory_space=pltpu.SMEM)] * 2 + [pl.BlockSpec(memory_space=pl.ANY)] * (len(operands) - 2),
        out_specs=[pl.BlockSpec(memory_space=space) for space in out_spaces],
        out_shape=out_shape,
        scratch_shapes=[
            pltpu.VMEM((rows, most * depth), tokens[0].dtype),
            pltpu.VMEM((slots, most * depth, width), weights[0].dtype),
            pltpu.VMEM((slots, rows, width) if n_accs else (slots, 8, 128), jnp.float32),
            pltpu.VMEM((2, 8, 128) if last else (2, rows, width), jnp.float32),
            pltpu.SemaphoreType.DMA((most,)),
            pltpu.SemaphoreType.DMA((slots, most)),
            pltpu.SemaphoreType.DMA((slots,)),
            pltpu.SemaphoreType.DMA((2,)),
            pltpu.SemaphoreType.DMA,
        ],
        compiler_params=pltpu.CompilerParams(vmem_limit_bytes=PHASE_VMEM * 2**20),
        cost_estimate=pl.CostEstimate(flops=0, bytes_accessed=0, transcendentals=0),
        name="phase",
    )(*operands)


def last_phase(tokens, weight, acc, out_dtype):
    part, depth = tokens[0].shape
    rows = part * len(tokens)
    total = weight.shape[1]
    width = tile_width(total)
    tiles = total // width
    n = len(tokens)

    def kernel(*refs):
        token_refs = refs[:n]
        w_ref, acc_ref, out_ref, tbuf, obuf, tsem, osem = refs[n:]

        def store(tile):
            at = pl.ds(tile * width, width)
            return pltpu.make_async_copy(obuf.at[:, at], out_ref.at[:, at], osem.at[tile])

        copies = [
            pltpu.make_async_copy(token_refs[k], tbuf.at[pl.ds(k * part, part)], tsem.at[k]) for k in range(n)
        ]
        for copy in copies:
            copy.start()
        for copy in copies:
            copy.wait()
        for tile in range(tiles):
            at = pl.ds(tile * width, width)
            product = jnp.dot(tbuf[...], w_ref[:, at], preferred_element_type=jnp.float32)
            obuf[:, at] = (acc_ref[:, at] + product).astype(out_dtype)
            store(tile).start()
        for tile in range(tiles):
            store(tile).wait()

    return pl.pallas_call(
        kernel,
        in_specs=[pl.BlockSpec(memory_space=pl.ANY)] * n + [pl.BlockSpec(memory_space=pltpu.VMEM)] * 2,
        out_specs=pl.BlockSpec(memory_space=pltpu.HBM),
        out_shape=jax.ShapeDtypeStruct((rows, total), out_dtype),
        scratch_shapes=[
            pltpu.VMEM((rows, depth), tokens[0].dtype),
            pltpu.VMEM((rows, total), out_dtype),
            pltpu.SemaphoreType.DMA((n,)),
            pltpu.SemaphoreType.DMA((tiles,)),
        ],
        compiler_params=pltpu.CompilerParams(vmem_limit_bytes=28 * 2**20),
        cost_estimate=pl.CostEstimate(flops=0, bytes_accessed=0, transcendentals=0),
        name="last_phase",
    )(*tokens, weight, acc)


def body(tokens, base_weight, delta_values, delta_index, delta_count, n_col):
    ring, order, meets = plan(n_col)
    half = n_col // 2
    ahead = [(ring[k], ring[(k + 1) % n_col]) for k in range(n_col)]
    behind = [(b, a) for a, b in ahead]
    swap = [(0, 1), (1, 0)]
    me = (lax.axis_index("col") * 2 + lax.axis_index("row")).astype(jnp.int32).reshape(1)
    index = delta_index.reshape(-1)
    count = delta_count.reshape(-1)
    devices = [row for col in meets for row in col]
    done = [set() for _ in devices]

    def run(want, acc, last, keep):
        had = [bool(d) for d in done]
        lists = [
            [(t, p) for t, p in enumerate(row) if t not in d and want(t, p)] for row, d in zip(devices, done)
        ]
        kinds = sorted({(len(items), int(h)) for items, h in zip(lists, had)})
        used_t = sorted({t for items in lists for t, _ in items})
        ends = [row[n_col - 1] for row in devices] if keep else []
        used_w = sorted({place[p][0] for items in lists for _, p in items} | {place[p][0] for p in ends})
        table = np.zeros((len(lists), 4 + 3 * max(max(k for k, _ in kinds), 1)), np.int32)
        for k, items in enumerate(lists):
            table[k, :2] = len(items), had[k]
            if keep:
                table[k, 2:4] = used_w.index(place[ends[k]][0]), place[ends[k]][1]
            for i, (t, p) in enumerate(items):
                table[k, 4 + 3 * i : 7 + 3 * i] = used_t.index(t), used_w.index(place[p][0]), place[p][1]
                done[k].add(t)
        return phase(
            me,
            jnp.asarray(table.reshape(-1)),
            kinds,
            [buffers[t] for t in used_t],
            [weights[w] for w in used_w],
            [k for k, w in enumerate(used_w) if w < PIN],
            [] if acc is None else [acc],
            last,
            keep,
        )

    fwd, bwd = lax.ppermute(tokens, "col", ahead), lax.ppermute(tokens, "col", behind)
    sets = [[0, half - 1], list(range(1, half - 1))]
    args = (me, order.reshape(2 * n_col, half).tolist(), index, count, base_weight, delta_values)
    local = [merge(*args, numbers, half, spare) for numbers, spare in zip(sets, (0, SPARE))]
    remote = [lax.ppermute(local[0], "row", swap), None]
    place = {}
    for w, numbers in enumerate(sets):
        for k, p in enumerate(numbers):
            place[p], place[half + p] = (w, k), (2 + w, k)
    buffers = [tokens]

    bounds = list(range(2, half - 1, 2)) + [half - 1]
    acc = None
    gate = list(local)
    for d in range(2, half + 1):
        (fwd,), (bwd,) = tie((fwd,), gate), tie((bwd,), gate)
        buffers += [fwd, bwd]
        if d == 2:
            (local[1],) = tie((local[1],), (fwd, bwd))
            remote[1] = lax.ppermute(local[1], "row", swap)
            weights = local + remote
        if d < half:
            next_fwd, next_bwd = lax.ppermute(fwd, "col", ahead), lax.ppermute(bwd, "col", behind)
        else:
            part = tokens.shape[0] // 2
            next_fwd, next_bwd = lax.ppermute(fwd[:part], "col", ahead), lax.ppermute(bwd[part:], "col", behind)
        gate = []
        if d == 2:
            weights = local + remote
            acc, kept = run(lambda t, p: t == 0, None, False, True)
            gate = [hbm(acc)]
        elif d - 1 in bounds:
            (acc,) = run(lambda t, p: t < 2 * d - 1, acc, d == half, False)
            gate = [hbm(acc)]
        fwd, bwd = next_fwd, next_bwd
    return last_phase([fwd, bwd], kept, acc, jnp.bfloat16)


def solution(mesh):
    spec = P(("tenant", "row"), "col")
    return jax.shard_map(
        functools.partial(body, n_col=mesh.shape["col"]),
        mesh=mesh,
        in_specs=(spec, P("row", "col"), spec, spec, spec),
        out_specs=spec,
        check_vma=False,
    )
```

```python
import functools

import jax
import jax.numpy as jnp
import numpy as np
from jax import lax
from jax.experimental import pallas as pl
from jax.experimental.pallas import tpu as pltpu
from jax.sharding import PartitionSpec as P

PHASE_VMEM = 24
SPARE = 16
PIN = 4


def ring_order(n):
    return list(range(0, n, 2)) + list(range(n - 1, 0, -2))


def plan(n):
    ring = ring_order(n)
    place = {c: k for k, c in enumerate(ring)}
    half = n // 2
    order = np.zeros((n, 2, half), np.int32)
    meets = np.zeros((n, 2, n), np.int32)
    for col in range(n):
        me = place[col]

        def dist(c):
            ahead = (place[c] - me) % n
            return min(ahead, n - ahead)

        def token_id(c):
            ahead = (place[c] - me) % n
            if ahead == 0:
                return 0
            if ahead == half:
                return n - 1
            return 2 * ahead if ahead < half else 2 * (n - ahead) - 1

        for h in range(2):
            chunks = sorted(range(h * half, (h + 1) * half), key=lambda c: (dist(c), c))
            order[col, h] = [c - h * half for c in chunks]
            for row in range(2):
                for j, c in enumerate(chunks):
                    meets[col, row, token_id(c)] = j if row == h else half + j
    return ring, order, meets.tolist()


def tie(values, after):
    n = len(values)

    def kernel(*refs):
        refs[-1][...] = jnp.zeros_like(refs[-1])

    return pl.pallas_call(
        kernel,
        in_specs=[pl.BlockSpec(memory_space=pl.ANY)] * (n + len(after)),
        out_specs=[pl.BlockSpec(memory_space=pl.ANY)] * n,
        out_shape=[jax.ShapeDtypeStruct(v.shape, v.dtype) for v in values],
        scratch_shapes=[pltpu.VMEM((8, 128), jnp.float32)],
        input_output_aliases={k: k for k in range(n)},
        compiler_params=pltpu.CompilerParams(vmem_limit_bytes=2**20),
        cost_estimate=pl.CostEstimate(flops=0, bytes_accessed=0, transcendentals=0),
        name="tie",
    )(*values, *after)


def hbm(x):
    return pltpu.with_memory_space_constraint(x, pltpu.HBM)


def merge(me, order, index, count, weight, values, numbers, total_pieces, spare):
    pieces = len(numbers)
    block = values.shape[1]
    blocks = weight.shape[0] // block // total_pieces
    width = weight.shape[1]
    col_blocks = width // block

    def kernel(me_ref, index_ref, count_ref, w_ref, values_ref, out_ref, vbuf, wsem, vsem):
        def chunk(p):
            found = jnp.int32(0)
            for k, chunks in enumerate(order):
                found = jnp.where(me_ref[0] == k, int(chunks[p]), found)
            return found

        value_copy = pltpu.make_async_copy(values_ref, vbuf, vsem)
        first = [chunk(p) * blocks for p in numbers]

        def copy(k):
            rows = pl.ds(pl.multiple_of((first[k // blocks] + k % blocks) * block, block), block)
            return pltpu.make_async_copy(w_ref.at[rows], out_ref.at[pl.ds(k * block, block)], wsem.at[k])

        value_copy.start()
        for k in range(pieces * blocks):
            copy(k).start()
        if spare:
            rest = out_ref.at[pl.ds(pieces * blocks * block, spare)]
            rest[...] = jnp.zeros((spare, width), out_ref.dtype)
        value_copy.wait()
        for k in range(pieces * blocks):
            copy(k).wait()

        def slot(s, carry):
            which = index_ref[s]
            row = which // col_blocks
            for p in range(pieces):
                row_here = row - first[p]

                @pl.when(jnp.logical_and(row_here >= 0, row_here < blocks))
                def _():
                    rows = pl.ds(pl.multiple_of((p * blocks + row_here) * block, block), block)
                    cols = pl.ds(pl.multiple_of((which - row * col_blocks) * block, block), block)
                    value = vbuf[pl.ds(pl.multiple_of(s * block, block), block), :]
                    old = out_ref[rows, cols]
                    out_ref[rows, cols] = (old.astype(jnp.float32) + value.astype(jnp.float32)).astype(out_ref.dtype)

            return carry

        lax.fori_loop(0, count_ref[0], slot, 0)

    shape = (pieces * blocks * block + spare, width)
    held = 2 * (shape[0] * width + values.shape[0] * values.shape[1])
    return pl.pallas_call(
        kernel,
        in_specs=[pl.BlockSpec(memory_space=pltpu.SMEM)] * 3 + [pl.BlockSpec(memory_space=pltpu.HBM)] * 2,
        out_specs=pl.BlockSpec(memory_space=pltpu.VMEM),
        out_shape=pltpu.VMEM(shape, weight.dtype),
        scratch_shapes=[
            pltpu.VMEM(values.shape, values.dtype),
            pltpu.SemaphoreType.DMA((pieces * blocks,)),
            pltpu.SemaphoreType.DMA,
        ],
        compiler_params=pltpu.CompilerParams(vmem_limit_bytes=held + 2**20),
        cost_estimate=pl.CostEstimate(flops=0, bytes_accessed=0, transcendentals=0),
        name="merge",
    )(me, index, count, hbm(weight), hbm(values))


def tile_width(total):
    return 512 if total % 512 == 0 else total


def phase(me, table, kinds, tokens, weights, pinned, occur, accs, last, keep):
    n_tokens, n_weights, n_accs = len(tokens), len(weights), len(accs)
    rows, depth = tokens[0].shape
    total = weights[0].shape[1]
    width = tile_width(total)
    tiles = total // width
    most = max(max(count for count, _ in kinds), 1)
    stride = 4 + 3 * most
    slots = 3 if most > 3 else 4

    def kernel(me_ref, table_ref, *refs):
        token_refs, refs = refs[:n_tokens], refs[n_tokens:]
        weight_refs, refs = refs[:n_weights], refs[n_weights:]
        acc_refs, refs = refs[:n_accs], refs[n_accs:]
        out_ref, refs = refs[0], refs[1:]
        if keep:
            kept_ref, refs = refs[0], refs[1:]
        tbuf, wbuf, abuf, obuf, tsem, wsem, asem, osem, ksem = refs
        base = me_ref[0] * stride

        def columns(tile):
            return pl.ds(pl.multiple_of(tile * width, 128), width)

        def token_copy(ref, i):
            return pltpu.make_async_copy(ref, tbuf.at[:, pl.ds(i * depth, depth)], tsem.at[i])

        def piece_rows(at):
            return pl.ds(pl.multiple_of(table_ref[at] * depth, depth), depth)

        def weight_copy(ref, rows_there, tile, i):
            slot = lax.rem(tile, slots)
            return pltpu.make_async_copy(
                ref.at[rows_there, columns(tile)], wbuf.at[slot, pl.ds(i * depth, depth)], wsem.at[slot, i]
            )

        def acc_copy(tile):
            slot = lax.rem(tile, slots)
            return pltpu.make_async_copy(acc_refs[0].at[:, columns(tile)], abuf.at[slot], asem.at[slot])

        def store(tile):
            slot = lax.rem(tile, 2)
            return pltpu.make_async_copy(obuf.at[slot], out_ref.at[:, columns(tile)], osem.at[slot])

        def fetch(tile, count, use_acc):
            for i in range(count):
                for w in occur[i][1]:

                    @pl.when(table_ref[base + 5 + 3 * i] == w)
                    def _():
                        weight_copy(weight_refs[w], piece_rows(base + 6 + 3 * i), tile, i).start()

            if use_acc:
                acc_copy(tile).start()

        def work(count, use_acc):
            for i in range(count):
                for t in occur[i][0]:

                    @pl.when(table_ref[base + 4 + 3 * i] == t)
                    def _():
                        token_copy(token_refs[t], i).start()

            fetch(jnp.int32(0), count, use_acc)
            for i in range(count):
                token_copy(token_refs[0], i).wait()

            def step(tile, carry):
                if keep:

                    @pl.when(tile == tiles // 2)
                    def _():
                        for w in range(n_weights):

                            @pl.when(table_ref[base + 2] == w)
                            def _():
                                pltpu.make_async_copy(weight_refs[w].at[piece_rows(base + 3)], kept_ref, ksem).start()

                slot = lax.rem(tile, slots)
                for i in range(count):
                    weight_copy(weight_refs[0], pl.ds(0, depth), tile, i).wait()
                if use_acc:
                    acc_copy(tile).wait()

                @pl.when(tile == 0)
                def _():
                    for later in range(1, min(slots - 1, tiles)):
                        fetch(jnp.int32(later), count, use_acc)

                @pl.when(tile + slots - 1 < tiles)
                def _():
                    fetch(tile + slots - 1, count, use_acc)

                deep = pl.ds(0, count * depth)
                value = jnp.dot(tbuf[:, deep], wbuf[slot, deep], preferred_element_type=jnp.float32)
                if use_acc:
                    value = value + abuf[slot]
                if last:
                    out_ref[:, columns(tile)] = value
                else:

                    @pl.when(tile >= 2)
                    def _():
                        store(tile - 2).wait()

                    obuf[lax.rem(tile, 2)] = value
                    store(tile).start()
                return carry

            lax.fori_loop(0, tiles, step, 0)
            if keep:
                pltpu.make_async_copy(weight_refs[0].at[pl.ds(0, depth)], kept_ref, ksem).wait()
            if not last:
                for tile in range(max(0, tiles - 2), tiles):
                    store(tile).wait()

        for count, use_acc in kinds:
            if count:

                @pl.when(jnp.logical_and(table_ref[base] == count, table_ref[base + 1] == use_acc))
                def _():
                    work(count, use_acc)

    place = pltpu.VMEM if last else pltpu.HBM
    out_shape = [place((rows, total), jnp.float32)]
    out_spaces = [place]
    if keep:
        out_shape.append(pltpu.VMEM((depth, total), weights[0].dtype))
        out_spaces.append(pltpu.VMEM)
    operands = [me, table] + list(tokens) + [hbm(w) if k in pinned else w for k, w in enumerate(weights)]
    operands += [hbm(a) for a in accs]
    return pl.pallas_call(
        kernel,
        in_specs=[pl.BlockSpec(memory_space=pltpu.SMEM)] * 2 + [pl.BlockSpec(memory_space=pl.ANY)] * (len(operands) - 2),
        out_specs=[pl.BlockSpec(memory_space=space) for space in out_spaces],
        out_shape=out_shape,
        scratch_shapes=[
            pltpu.VMEM((rows, most * depth), tokens[0].dtype),
            pltpu.VMEM((slots, most * depth, width), weights[0].dtype),
            pltpu.VMEM((slots, rows, width) if n_accs else (slots, 8, 128), jnp.float32),
            pltpu.VMEM((2, 8, 128) if last else (2, rows, width), jnp.float32),
            pltpu.SemaphoreType.DMA((most,)),
            pltpu.SemaphoreType.DMA((slots, most)),
            pltpu.SemaphoreType.DMA((slots,)),
            pltpu.SemaphoreType.DMA((2,)),
            pltpu.SemaphoreType.DMA,
        ],
        compiler_params=pltpu.CompilerParams(vmem_limit_bytes=PHASE_VMEM * 2**20),
        cost_estimate=pl.CostEstimate(flops=0, bytes_accessed=0, transcendentals=0),
        name="phase",
    )(*operands)


def last_phase(tokens, weight, acc, out_dtype):
    part, depth = tokens[0].shape
    rows = part * len(tokens)
    total = weight.shape[1]
    width = tile_width(total)
    tiles = total // width
    n = len(tokens)

    def kernel(*refs):
        token_refs = refs[:n]
        w_ref, acc_ref, out_ref, tbuf, obuf, tsem, osem = refs[n:]

        def store(tile):
            at = pl.ds(tile * width, width)
            return pltpu.make_async_copy(obuf.at[:, at], out_ref.at[:, at], osem.at[tile])

        copies = [
            pltpu.make_async_copy(token_refs[k], tbuf.at[pl.ds(k * part, part)], tsem.at[k]) for k in range(n)
        ]
        for copy in copies:
            copy.start()
        for copy in copies:
            copy.wait()
        for tile in range(tiles):
            at = pl.ds(tile * width, width)
            product = jnp.dot(tbuf[...], w_ref[:, at], preferred_element_type=jnp.float32)
            obuf[:, at] = (acc_ref[:, at] + product).astype(out_dtype)
            store(tile).start()
        for tile in range(tiles):
            store(tile).wait()

    return pl.pallas_call(
        kernel,
        in_specs=[pl.BlockSpec(memory_space=pl.ANY)] * n + [pl.BlockSpec(memory_space=pltpu.VMEM)] * 2,
        out_specs=pl.BlockSpec(memory_space=pltpu.HBM),
        out_shape=jax.ShapeDtypeStruct((rows, total), out_dtype),
        scratch_shapes=[
            pltpu.VMEM((rows, depth), tokens[0].dtype),
            pltpu.VMEM((rows, total), out_dtype),
            pltpu.SemaphoreType.DMA((n,)),
            pltpu.SemaphoreType.DMA((tiles,)),
        ],
        compiler_params=pltpu.CompilerParams(vmem_limit_bytes=28 * 2**20),
        cost_estimate=pl.CostEstimate(flops=0, bytes_accessed=0, transcendentals=0),
        name="last_phase",
    )(*tokens, weight, acc)


def body(tokens, base_weight, delta_values, delta_index, delta_count, n_col):
    ring, order, meets = plan(n_col)
    half = n_col // 2
    ahead = [(ring[k], ring[(k + 1) % n_col]) for k in range(n_col)]
    behind = [(b, a) for a, b in ahead]
    swap = [(0, 1), (1, 0)]
    me = (lax.axis_index("col") * 2 + lax.axis_index("row")).astype(jnp.int32).reshape(1)
    index = delta_index.reshape(-1)
    count = delta_count.reshape(-1)
    devices = [row for col in meets for row in col]
    done = [set() for _ in devices]

    def run(want, acc, last, keep):
        had = [bool(d) for d in done]
        lists = [
            [(t, p) for t, p in enumerate(row) if t not in d and want(t, p)] for row, d in zip(devices, done)
        ]
        kinds = sorted({(len(items), int(h)) for items, h in zip(lists, had)})
        used_t = sorted({t for items in lists for t, _ in items})
        ends = [row[n_col - 1] for row in devices] if keep else []
        used_w = sorted({place[p][0] for items in lists for _, p in items} | {place[p][0] for p in ends})
        table = np.zeros((len(lists), 4 + 3 * max(max(k for k, _ in kinds), 1)), np.int32)
        for k, items in enumerate(lists):
            table[k, :2] = len(items), had[k]
            if keep:
                table[k, 2:4] = used_w.index(place[ends[k]][0]), place[ends[k]][1]
            for i, (t, p) in enumerate(items):
                table[k, 4 + 3 * i : 7 + 3 * i] = used_t.index(t), used_w.index(place[p][0]), place[p][1]
                done[k].add(t)
        return phase(
            me,
            jnp.asarray(table.reshape(-1)),
            kinds,
            [buffers[t] for t in used_t],
            [weights[w] for w in used_w],
            [k for k, w in enumerate(used_w) if w < PIN],
            [
                [sorted({int(row[at + 3 * i]) for row in table if row[0] > i}) for at in (4, 5)]
                for i in range(max(k for k, _ in kinds))
            ],
            [] if acc is None else [acc],
            last,
            keep,
        )

    fwd, bwd = lax.ppermute(tokens, "col", ahead), lax.ppermute(tokens, "col", behind)
    sets = [[0, half - 1], list(range(1, half - 1))]
    args = (me, order.reshape(2 * n_col, half).tolist(), index, count, base_weight, delta_values)
    local = [merge(*args, numbers, half, spare) for numbers, spare in zip(sets, (0, SPARE))]
    remote = [lax.ppermute(local[0], "row", swap), None]
    place = {}
    for w, numbers in enumerate(sets):
        for k, p in enumerate(numbers):
            place[p], place[half + p] = (w, k), (2 + w, k)
    buffers = [tokens]

    bounds = list(range(2, half - 1, 2)) + [half - 1]
    acc = None
    gate = list(local)
    for d in range(2, half + 1):
        (fwd,), (bwd,) = tie((fwd,), gate), tie((bwd,), gate)
        buffers += [fwd, bwd]
        if d == 2:
            (local[1],) = tie((local[1],), (fwd, bwd))
            remote[1] = lax.ppermute(local[1], "row", swap)
            weights = local + remote
        if d < half:
            next_fwd, next_bwd = lax.ppermute(fwd, "col", ahead), lax.ppermute(bwd, "col", behind)
        else:
            part = tokens.shape[0] // 2
            next_fwd, next_bwd = lax.ppermute(fwd[:part], "col", ahead), lax.ppermute(bwd[part:], "col", behind)
        gate = []
        if d == 2:
            weights = local + remote
            acc, kept = run(lambda t, p: t == 0, None, False, True)
            gate = [hbm(acc)]
        elif d - 1 in bounds:
            (acc,) = run(lambda t, p: t < 2 * d - 1, acc, d == half, False)
            gate = [hbm(acc)]
        fwd, bwd = next_fwd, next_bwd
    return last_phase([fwd, bwd], kept, acc, jnp.bfloat16)


def solution(mesh):
    spec = P(("tenant", "row"), "col")
    return jax.shard_map(
        functools.partial(body, n_col=mesh.shape["col"]),
        mesh=mesh,
        in_specs=(spec, P("row", "col"), spec, spec, spec),
        out_specs=spec,
        check_vma=False,
    )
```

```python
import functools

import jax
import jax.numpy as jnp
import numpy as np
from jax import lax
from jax.experimental import pallas as pl
from jax.experimental.pallas import tpu as pltpu
from jax.sharding import PartitionSpec as P

PHASE_VMEM = 24
SPARE = 16
PIN = 4


def ring_order(n):
    return list(range(0, n, 2)) + list(range(n - 1, 0, -2))


def plan(n):
    ring = ring_order(n)
    place = {c: k for k, c in enumerate(ring)}
    half = n // 2
    order = np.zeros((n, 2, half), np.int32)
    meets = np.zeros((n, 2, n), np.int32)
    for col in range(n):
        me = place[col]

        def dist(c):
            ahead = (place[c] - me) % n
            return min(ahead, n - ahead)

        def token_id(c):
            ahead = (place[c] - me) % n
            if ahead == 0:
                return 0
            if ahead == half:
                return n - 1
            return 2 * ahead if ahead < half else 2 * (n - ahead) - 1

        for h in range(2):
            chunks = sorted(range(h * half, (h + 1) * half), key=lambda c: (dist(c), c))
            order[col, h] = [c - h * half for c in chunks]
            for row in range(2):
                for j, c in enumerate(chunks):
                    meets[col, row, token_id(c)] = j if row == h else half + j
    return ring, order, meets.tolist()


def tie(values, after):
    n = len(values)

    def kernel(*refs):
        refs[-1][...] = jnp.zeros_like(refs[-1])

    return pl.pallas_call(
        kernel,
        in_specs=[pl.BlockSpec(memory_space=pl.ANY)] * (n + len(after)),
        out_specs=[pl.BlockSpec(memory_space=pl.ANY)] * n,
        out_shape=[jax.ShapeDtypeStruct(v.shape, v.dtype) for v in values],
        scratch_shapes=[pltpu.VMEM((8, 128), jnp.float32)],
        input_output_aliases={k: k for k in range(n)},
        compiler_params=pltpu.CompilerParams(vmem_limit_bytes=2**20),
        cost_estimate=pl.CostEstimate(flops=0, bytes_accessed=0, transcendentals=0),
        name="tie",
    )(*values, *after)


def hbm(x):
    return pltpu.with_memory_space_constraint(x, pltpu.HBM)


def merge(me, order, index, count, weight, values, numbers, total_pieces, spare):
    pieces = len(numbers)
    block = values.shape[1]
    blocks = weight.shape[0] // block // total_pieces
    width = weight.shape[1]
    col_blocks = width // block

    def kernel(me_ref, index_ref, count_ref, w_ref, values_ref, out_ref, vbuf, wsem, vsem):
        def chunk(p):
            found = jnp.int32(0)
            for k, chunks in enumerate(order):
                found = jnp.where(me_ref[0] == k, int(chunks[p]), found)
            return found

        value_copy = pltpu.make_async_copy(values_ref, vbuf, vsem)
        first = [chunk(p) * blocks for p in numbers]

        def copy(k):
            rows = pl.ds(pl.multiple_of((first[k // blocks] + k % blocks) * block, block), block)
            return pltpu.make_async_copy(w_ref.at[rows], out_ref.at[pl.ds(k * block, block)], wsem.at[k])

        value_copy.start()
        for k in range(pieces * blocks):
            copy(k).start()
        if spare:
            rest = out_ref.at[pl.ds(pieces * blocks * block, spare)]
            rest[...] = jnp.zeros((spare, width), out_ref.dtype)
        for p in range(pieces):
            for k in range(p * blocks, (p + 1) * blocks):
                copy(k).wait()
            if p == 0:
                value_copy.wait()

            def slot(s, carry):
                which = index_ref[s]
                col = which - first[p] * col_blocks

                @pl.when(jnp.logical_and(col >= 0, col < blocks * col_blocks))
                def _():
                    row_here = col // col_blocks
                    rows = pl.ds(pl.multiple_of((p * blocks + row_here) * block, block), block)
                    cols = pl.ds(pl.multiple_of((col - row_here * col_blocks) * block, block), block)
                    value = vbuf[pl.ds(pl.multiple_of(s * block, block), block), :]
                    old = out_ref[rows, cols]
                    out_ref[rows, cols] = (old.astype(jnp.float32) + value.astype(jnp.float32)).astype(out_ref.dtype)

                return carry

            lax.fori_loop(0, count_ref[0], slot, 0)

    shape = (pieces * blocks * block + spare, width)
    held = 2 * (shape[0] * width + values.shape[0] * values.shape[1])
    return pl.pallas_call(
        kernel,
        in_specs=[pl.BlockSpec(memory_space=pltpu.SMEM)] * 3 + [pl.BlockSpec(memory_space=pltpu.HBM)] * 2,
        out_specs=pl.BlockSpec(memory_space=pltpu.VMEM),
        out_shape=pltpu.VMEM(shape, weight.dtype),
        scratch_shapes=[
            pltpu.VMEM(values.shape, values.dtype),
            pltpu.SemaphoreType.DMA((pieces * blocks,)),
            pltpu.SemaphoreType.DMA,
        ],
        compiler_params=pltpu.CompilerParams(vmem_limit_bytes=held + 2**20),
        cost_estimate=pl.CostEstimate(flops=0, bytes_accessed=0, transcendentals=0),
        name="merge",
    )(me, index, count, hbm(weight), hbm(values))


def tile_width(total):
    return 512 if total % 512 == 0 else total


def phase(me, table, kinds, tokens, weights, pinned, occur, accs, last, keep):
    n_tokens, n_weights, n_accs = len(tokens), len(weights), len(accs)
    rows, depth = tokens[0].shape
    total = weights[0].shape[1]
    width = tile_width(total)
    tiles = total // width
    most = max(max(count for count, _ in kinds), 1)
    stride = 4 + 3 * most
    slots = 3 if most > 3 else 4

    def kernel(me_ref, table_ref, *refs):
        token_refs, refs = refs[:n_tokens], refs[n_tokens:]
        weight_refs, refs = refs[:n_weights], refs[n_weights:]
        acc_refs, refs = refs[:n_accs], refs[n_accs:]
        out_ref, refs = refs[0], refs[1:]
        if keep:
            kept_ref, refs = refs[0], refs[1:]
        tbuf, wbuf, abuf, obuf, tsem, wsem, asem, osem, ksem = refs
        base = me_ref[0] * stride

        def columns(tile):
            return pl.ds(pl.multiple_of(tile * width, 128), width)

        def token_copy(ref, i):
            return pltpu.make_async_copy(ref, tbuf.at[:, pl.ds(i * depth, depth)], tsem.at[i])

        def piece_rows(at):
            return pl.ds(pl.multiple_of(table_ref[at] * depth, depth), depth)

        def weight_copy(ref, rows_there, tile, i):
            slot = lax.rem(tile, slots)
            return pltpu.make_async_copy(
                ref.at[rows_there, columns(tile)], wbuf.at[slot, pl.ds(i * depth, depth)], wsem.at[slot, i]
            )

        def acc_copy(tile):
            slot = lax.rem(tile, slots)
            return pltpu.make_async_copy(acc_refs[0].at[:, columns(tile)], abuf.at[slot], asem.at[slot])

        def store(tile):
            slot = lax.rem(tile, 2)
            return pltpu.make_async_copy(obuf.at[slot], out_ref.at[:, columns(tile)], osem.at[slot])

        def fetch(tile, count, use_acc):
            for i in range(count):
                for w in occur[i][1]:

                    @pl.when(table_ref[base + 5 + 3 * i] == w)
                    def _():
                        weight_copy(weight_refs[w], piece_rows(base + 6 + 3 * i), tile, i).start()

            if use_acc:
                acc_copy(tile).start()

        def work(count, use_acc):
            for i in range(count):
                for t in occur[i][0]:

                    @pl.when(table_ref[base + 4 + 3 * i] == t)
                    def _():
                        token_copy(token_refs[t], i).start()

            fetch(jnp.int32(0), count, use_acc)
            for i in range(count):
                token_copy(token_refs[0], i).wait()

            def step(tile, carry):
                if keep:

                    @pl.when(tile == tiles // 2)
                    def _():
                        for w in range(n_weights):

                            @pl.when(table_ref[base + 2] == w)
                            def _():
                                pltpu.make_async_copy(weight_refs[w].at[piece_rows(base + 3)], kept_ref, ksem).start()

                slot = lax.rem(tile, slots)
                for i in range(count):
                    weight_copy(weight_refs[0], pl.ds(0, depth), tile, i).wait()
                if use_acc:
                    acc_copy(tile).wait()

                @pl.when(tile == 0)
                def _():
                    for later in range(1, min(slots - 1, tiles)):
                        fetch(jnp.int32(later), count, use_acc)

                @pl.when(tile + slots - 1 < tiles)
                def _():
                    fetch(tile + slots - 1, count, use_acc)

                deep = pl.ds(0, count * depth)
                value = jnp.dot(tbuf[:, deep], wbuf[slot, deep], preferred_element_type=jnp.float32)
                if use_acc:
                    value = value + abuf[slot]
                if last:
                    out_ref[:, columns(tile)] = value
                else:

                    @pl.when(tile >= 2)
                    def _():
                        store(tile - 2).wait()

                    obuf[lax.rem(tile, 2)] = value
                    store(tile).start()
                return carry

            lax.fori_loop(0, tiles, step, 0)
            if keep:
                pltpu.make_async_copy(weight_refs[0].at[pl.ds(0, depth)], kept_ref, ksem).wait()
            if not last:
                for tile in range(max(0, tiles - 2), tiles):
                    store(tile).wait()

        for count, use_acc in kinds:
            if count:

                @pl.when(jnp.logical_and(table_ref[base] == count, table_ref[base + 1] == use_acc))
                def _():
                    work(count, use_acc)

    place = pltpu.VMEM if last else pltpu.HBM
    out_shape = [place((rows, total), jnp.float32)]
    out_spaces = [place]
    if keep:
        out_shape.append(pltpu.VMEM((depth, total), weights[0].dtype))
        out_spaces.append(pltpu.VMEM)
    operands = [me, table] + list(tokens) + [hbm(w) if k in pinned else w for k, w in enumerate(weights)]
    operands += [hbm(a) for a in accs]
    return pl.pallas_call(
        kernel,
        in_specs=[pl.BlockSpec(memory_space=pltpu.SMEM)] * 2 + [pl.BlockSpec(memory_space=pl.ANY)] * (len(operands) - 2),
        out_specs=[pl.BlockSpec(memory_space=space) for space in out_spaces],
        out_shape=out_shape,
        scratch_shapes=[
            pltpu.VMEM((rows, most * depth), tokens[0].dtype),
            pltpu.VMEM((slots, most * depth, width), weights[0].dtype),
            pltpu.VMEM((slots, rows, width) if n_accs else (slots, 8, 128), jnp.float32),
            pltpu.VMEM((2, 8, 128) if last else (2, rows, width), jnp.float32),
            pltpu.SemaphoreType.DMA((most,)),
            pltpu.SemaphoreType.DMA((slots, most)),
            pltpu.SemaphoreType.DMA((slots,)),
            pltpu.SemaphoreType.DMA((2,)),
            pltpu.SemaphoreType.DMA,
        ],
        compiler_params=pltpu.CompilerParams(vmem_limit_bytes=PHASE_VMEM * 2**20),
        cost_estimate=pl.CostEstimate(flops=0, bytes_accessed=0, transcendentals=0),
        name="phase",
    )(*operands)


def last_phase(tokens, weight, acc, out_dtype):
    part, depth = tokens[0].shape
    rows = part * len(tokens)
    total = weight.shape[1]
    width = tile_width(total)
    tiles = total // width
    n = len(tokens)

    def kernel(*refs):
        token_refs = refs[:n]
        w_ref, acc_ref, out_ref, tbuf, obuf, tsem, osem = refs[n:]

        def store(tile):
            at = pl.ds(tile * width, width)
            return pltpu.make_async_copy(obuf.at[:, at], out_ref.at[:, at], osem.at[tile])

        copies = [
            pltpu.make_async_copy(token_refs[k], tbuf.at[pl.ds(k * part, part)], tsem.at[k]) for k in range(n)
        ]
        for copy in copies:
            copy.start()
        for copy in copies:
            copy.wait()
        for tile in range(tiles):
            at = pl.ds(tile * width, width)
            product = jnp.dot(tbuf[...], w_ref[:, at], preferred_element_type=jnp.float32)
            obuf[:, at] = (acc_ref[:, at] + product).astype(out_dtype)
            store(tile).start()
        for tile in range(tiles):
            store(tile).wait()

    return pl.pallas_call(
        kernel,
        in_specs=[pl.BlockSpec(memory_space=pl.ANY)] * n + [pl.BlockSpec(memory_space=pltpu.VMEM)] * 2,
        out_specs=pl.BlockSpec(memory_space=pltpu.HBM),
        out_shape=jax.ShapeDtypeStruct((rows, total), out_dtype),
        scratch_shapes=[
            pltpu.VMEM((rows, depth), tokens[0].dtype),
            pltpu.VMEM((rows, total), out_dtype),
            pltpu.SemaphoreType.DMA((n,)),
            pltpu.SemaphoreType.DMA((tiles,)),
        ],
        compiler_params=pltpu.CompilerParams(vmem_limit_bytes=28 * 2**20),
        cost_estimate=pl.CostEstimate(flops=0, bytes_accessed=0, transcendentals=0),
        name="last_phase",
    )(*tokens, weight, acc)


def body(tokens, base_weight, delta_values, delta_index, delta_count, n_col):
    ring, order, meets = plan(n_col)
    half = n_col // 2
    ahead = [(ring[k], ring[(k + 1) % n_col]) for k in range(n_col)]
    behind = [(b, a) for a, b in ahead]
    swap = [(0, 1), (1, 0)]
    me = (lax.axis_index("col") * 2 + lax.axis_index("row")).astype(jnp.int32).reshape(1)
    index = delta_index.reshape(-1)
    count = delta_count.reshape(-1)
    devices = [row for col in meets for row in col]
    done = [set() for _ in devices]

    def run(want, acc, last, keep):
        had = [bool(d) for d in done]
        lists = [
            [(t, p) for t, p in enumerate(row) if t not in d and want(t, p)] for row, d in zip(devices, done)
        ]
        kinds = sorted({(len(items), int(h)) for items, h in zip(lists, had)})
        used_t = sorted({t for items in lists for t, _ in items})
        ends = [row[n_col - 1] for row in devices] if keep else []
        used_w = sorted({place[p][0] for items in lists for _, p in items} | {place[p][0] for p in ends})
        table = np.zeros((len(lists), 4 + 3 * max(max(k for k, _ in kinds), 1)), np.int32)
        for k, items in enumerate(lists):
            table[k, :2] = len(items), had[k]
            if keep:
                table[k, 2:4] = used_w.index(place[ends[k]][0]), place[ends[k]][1]
            for i, (t, p) in enumerate(items):
                table[k, 4 + 3 * i : 7 + 3 * i] = used_t.index(t), used_w.index(place[p][0]), place[p][1]
                done[k].add(t)
        return phase(
            me,
            jnp.asarray(table.reshape(-1)),
            kinds,
            [buffers[t] for t in used_t],
            [weights[w] for w in used_w],
            [k for k, w in enumerate(used_w) if w < PIN],
            [
                [sorted({int(row[at + 3 * i]) for row in table if row[0] > i}) for at in (4, 5)]
                for i in range(max(k for k, _ in kinds))
            ],
            [] if acc is None else [acc],
            last,
            keep,
        )

    fwd, bwd = lax.ppermute(tokens, "col", ahead), lax.ppermute(tokens, "col", behind)
    sets = [[0, half - 1], list(range(1, half - 1))]
    args = (me, order.reshape(2 * n_col, half).tolist(), index, count, base_weight, delta_values)
    local = [merge(*args, numbers, half, spare) for numbers, spare in zip(sets, (0, SPARE))]
    remote = [lax.ppermute(local[0], "row", swap), None]
    place = {}
    for w, numbers in enumerate(sets):
        for k, p in enumerate(numbers):
            place[p], place[half + p] = (w, k), (2 + w, k)
    buffers = [tokens]

    bounds = list(range(2, half - 1, 2)) + [half - 1]
    acc = None
    gate = list(local)
    for d in range(2, half + 1):
        (fwd,), (bwd,) = tie((fwd,), gate), tie((bwd,), gate)
        buffers += [fwd, bwd]
        if d == 2:
            (local[1],) = tie((local[1],), (fwd, bwd))
            remote[1] = lax.ppermute(local[1], "row", swap)
            weights = local + remote
        if d < half:
            next_fwd, next_bwd = lax.ppermute(fwd, "col", ahead), lax.ppermute(bwd, "col", behind)
        else:
            part = tokens.shape[0] // 2
            next_fwd, next_bwd = lax.ppermute(fwd[:part], "col", ahead), lax.ppermute(bwd[part:], "col", behind)
        gate = []
        if d == 2:
            weights = local + remote
            acc, kept = run(lambda t, p: t == 0, None, False, True)
            gate = [hbm(acc)]
        elif d - 1 in bounds:
            (acc,) = run(lambda t, p: t < 2 * d - 1, acc, d == half, False)
            gate = [hbm(acc)]
        fwd, bwd = next_fwd, next_bwd
    return last_phase([fwd, bwd], kept, acc, jnp.bfloat16)


def solution(mesh):
    spec = P(("tenant", "row"), "col")
    return jax.shard_map(
        functools.partial(body, n_col=mesh.shape["col"]),
        mesh=mesh,
        in_specs=(spec, P("row", "col"), spec, spec, spec),
        out_specs=spec,
        check_vma=False,
    )
```
